32 devices in a mesh: rows: 8 (over z, x), feat: 4 (over y, core).
Axes of the slice: x: 2, y: 2, z: 4, core: 2. Of those that a mesh axis runs over, the one named last changes fastest.
Arguments:
- edge_feats: bfloat16 [8192, 256], P(('rows', 'feat')), may hold values from -6 to 6
- edge_owner: int32 [8192, 1], P(('rows', 'feat')), may hold values from 0 to 7; in each aligned block of 256 rows (0 to 255, 256 to 511, ...) at most 64 rows name the same one
- src_local: int32 [8192], P(('rows', 'feat')), may hold values from 0 to 63
- band_slot: int32 [8192], P(('rows', 'feat')), may hold values from 0 to 8
- dst_local: int32 [8192], P(('rows', 'feat')), may hold values from 0 to 7
- w_first: bfloat16 [256, 256], replicated, may hold values from -0.375 to 0.375
- w_second: bfloat16 [256, 256], replicated, may hold values from -0.375 to 0.375
- w_third: bfloat16 [256, 256], replicated, may hold values from -0.375 to 0.375
Outputs:
- density: float32 [64, 9, 128, 128], P('rows', None, 'feat')
The draws below stay inside these ranges and needn't reach their ends.
Inputs may be any that keep to these rules, and one draw needn't show every extreme that they name: `edge_owner`: among the 256 edges of one device (aligned blocks of rows), no index of rows is named more than 64 times, a bound that some block reaches.
All inputs are finite; a program needn't handle non-finite values.
Results may differ from the reference program's by a relative error of at most 0.0014.
Values sent between devices are 32-bit elements; how exact they have to be, the bound alone decides.
A program may use at most 64 MiB of HBM per device.

```python
import math
import jax
import jax.numpy as jnp
import numpy as np
from jax import lax

F = 256
BLOCK = 16
TILE = 128
BAND = 9
TILE_DEV = 8
EDGE_DEV = 256
CAP = 64
BPT = 8
TILES = 64
EDGES = 8192
N_ROWS = 8
N_FEAT = 4


def with_ends(drawn, key, low, largest):
    dims = drawn.shape
    place = [jax.random.randint(jax.random.fold_in(key, axis), (), 0, dims[axis]) for axis in range(len(dims))]
    drawn = drawn.at[tuple(place)].set(low)
    longest = dims.index(max(dims))
    place[longest] = (place[longest] + 1) % dims[longest]
    return drawn.at[tuple(place)].set(largest)


def shard_levels(rng, dims, split, low, largest):
    def one(axis_at, shards_of):
        draws = jax.random.uniform(jax.random.fold_in(jax.random.fold_in(rng, 6), axis_at), (shards_of,), jnp.float32, low / len(split), largest / len(split))
        return jnp.repeat(jnp.exp(draws), dims[axis_at] // shards_of).reshape((-1,) + (1,) * (len(dims) - axis_at - 1))

    factor_of = one(*split[0])
    for cut in split[1:]:
        factor_of = factor_of * one(*cut)
    return factor_of


def routed_block(rng, own, number, rows, amount, top, limit, lean):
    sequence = jax.random.permutation(rng, amount)
    heavy_load, usual = shares(amount, rows * top, limit, lean, True), shares(amount, rows * top, limit, lean, False)
    places = jnp.arange(amount)

    def named(tallies, rotation):
        used = int((tallies > 0).sum())
        fixed = max(1, used // 4)
        moved = fixed + (places - fixed + rotation * (used - fixed)) % max(1, amount - fixed)
        return jnp.zeros((amount,), jnp.int32).at[sequence[jnp.where(places < fixed, places, moved)]].set(jnp.asarray(tallies, jnp.int32))

    tallies = jnp.where(number % 4 == 0, named(heavy_load, number // 4), named(usual, number - number // 4 - 1))
    mixed = jax.random.permutation(jax.random.fold_in(own, 3), amount)
    source_of, receiver = mixed[0:amount // 2 * 2:2], mixed[1:amount // 2 * 2:2]
    room = jnp.minimum(tallies[source_of] - 1, limit - tallies[receiver]) // 2
    room = jnp.where((source_of == sequence[0]) | (receiver == sequence[0]) | (tallies[receiver] == 0), 0, jnp.maximum(room, 0))
    moved = jax.random.randint(jax.random.fold_in(own, 4), (amount // 2,), 0, 1 << 20) % (room + 1)
    tallies = tallies.at[source_of].add(-moved).at[receiver].add(moved)
    items = jnp.searchsorted(jnp.cumsum(tallies), jnp.arange(rows * top), side="right").astype(jnp.int32)
    listing = items.reshape(top, rows).T
    listing = listing[jax.random.permutation(jax.random.fold_in(own, 1), rows)]
    rotation = jax.random.randint(jax.random.fold_in(own, 2), (rows, 1), 0, top)
    return jnp.take_along_axis(listing, (jnp.arange(top)[None, :] + rotation) % top, axis=1)


def shares(count, total, reach, slope, full):
    loads = [(1 << 20) // math.isqrt(rank ** slope) + 1 for rank in range(1, count + 1)]
    largest = reach if full else min(reach, max(-(-total // count), total * loads[0] // sum(loads)))
    least = 1 if total - largest >= count - 1 else 0
    counts, rest = [largest] + [least] * (count - 1), total - largest - least * (count - 1)
    while rest > 0:
        movable = [i for i in range(1, count) if counts[i] < largest] or [i for i in range(1, count) if counts[i] < reach]
        pool, remaining = sum([loads[i] for i in movable]), rest
        for i in movable:
            extra = min(reach - counts[i], max(1, remaining * loads[i] // pool), rest)
            counts[i] = counts[i] + extra
            rest = rest - extra
    return np.array(counts)


def normal_values(rng, shape, spread, reach, pieces=(), kind=jnp.bfloat16):
    result = spread * jax.random.normal(rng, shape, jnp.float32)
    if pieces:
        result = result * shard_levels(rng, shape, pieces, -0.22, 0.18)
    return jnp.clip(result, -reach, reach).astype(kind)


def setup_inputs(seed: int = 0) -> dict:
    keys = jax.random.split(jax.random.key(seed), 9)
    edge_feats = normal_values(keys[0], (EDGES, F), 1.0, 6.0, ((0, 32),))
    edge_owner_keys = jax.random.split(jax.random.fold_in(keys[1], 1), EDGES // EDGE_DEV)
    edge_owner_turns = jax.random.permutation(jax.random.fold_in(keys[1], 3), EDGES // EDGE_DEV)
    edge_owner = jax.vmap(lambda own, number: routed_block(jax.random.fold_in(keys[1], 2), own, number, EDGE_DEV, N_ROWS, 1, CAP, 2))(edge_owner_keys, edge_owner_turns).reshape((EDGES, 1))
    src_local = with_ends(jax.random.randint(keys[2], (EDGES,), 0, TILE_DEV * BPT), jax.random.fold_in(keys[2], 1), 0, (TILE_DEV * BPT) - 1).astype(jnp.int32)
    band_slot = with_ends(jax.random.randint(keys[3], (EDGES,), 0, BAND), jax.random.fold_in(keys[3], 1), 0, BAND - 1).astype(jnp.int32)
    dst_local = with_ends(jax.random.randint(keys[4], (EDGES,), 0, BPT), jax.random.fold_in(keys[4], 1), 0, BPT - 1).astype(jnp.int32)
    w_first = normal_values(keys[5], (F, F), F ** -0.5, 0.375)
    w_second = normal_values(keys[6], (F, F), F ** -0.5, 0.375)
    w_third = normal_values(keys[7], (F, BLOCK * BLOCK), F ** -0.5, 0.375)
    return dict(edge_feats=edge_feats, edge_owner=edge_owner, src_local=src_local, band_slot=band_slot, dst_local=dst_local, w_first=w_first, w_second=w_second, w_third=w_third)


def edge_values(edge_feats, w_first, w_second, w_third):
    hidden_one = jax.nn.silu(jnp.dot(edge_feats, w_first, preferred_element_type=jnp.float32)).astype(jnp.bfloat16)
    hidden_two = jax.nn.silu(jnp.dot(hidden_one, w_second, preferred_element_type=jnp.float32)).astype(jnp.bfloat16)
    return jnp.dot(hidden_two, w_third, preferred_element_type=jnp.float32)

def band_product(left_band, right_band):
    half_band = BAND // 2
    summed = jnp.zeros(left_band.shape, jnp.float32)
    for offset in range(BAND):
        shifted = jnp.roll(right_band, -(offset - half_band), axis=0)
        lower_slot = max(0, offset - half_band)
        upper_slot = min(BAND, offset + half_band + 1)
        product = jnp.einsum('irm,icmk->icrk', left_band[:, offset], shifted[:, lower_slot - offset + half_band:upper_slot - offset + half_band], precision=lax.Precision.HIGHEST)
        summed = summed.at[:, lower_slot:upper_slot].add(product)
    return summed

def reference(edge_feats, edge_owner, src_local, band_slot, dst_local, w_first, w_second, w_third):
    group_cols = BLOCK // N_FEAT
    col_width = TILE // N_FEAT
    blocks_tile = TILE // BLOCK
    half_band = BAND // 2
    values = edge_values(edge_feats, w_first, w_second, w_third)
    entries = jnp.arange(BLOCK * BLOCK, dtype=jnp.int32)
    group_index = entries // (BLOCK * group_cols)
    component = entries // group_cols % BLOCK
    unit_col = entries % group_cols
    tile_row = edge_owner[:, 0] * TILE_DEV + src_local // blocks_tile
    src_block = src_local % blocks_tile
    row_pos = (component // group_cols)[None, :] * col_width + src_block[:, None] * group_cols + (component % group_cols)[None, :]
    col_pos = group_index[None, :] * col_width + dst_local[:, None] * group_cols + unit_col[None, :]
    flat_index = ((tile_row * BAND + band_slot)[:, None] * TILE + row_pos) * TILE + col_pos
    hamil = jnp.zeros((TILES * BAND * TILE * TILE,), jnp.float32)
    hamil = hamil.at[flat_index.reshape(-1)].add(values.reshape(-1)).reshape(TILES, BAND, TILE, TILE)
    partner = jnp.stack([jnp.roll(hamil[:, BAND - 1 - slot_index], -(slot_index - half_band), axis=0) for slot_index in range(BAND)], axis=1)
    degree = N_FEAT * EDGE_DEV / (TILE_DEV * blocks_tile)
    gamma = 0.5 / math.sqrt(2.0 * BLOCK * degree)
    start = 0.5 * gamma * (hamil + jnp.swapaxes(partner, 2, 3))
    start = start.at[:, half_band].add(0.5 * jnp.eye(TILE, dtype=jnp.float32))
    squared = band_product(start, start)
    purified = 2.0 * squared - band_product(squared, squared)
    return jnp.swapaxes(purified, 2, 3)
```

```python
import functools
import math

import jax
import jax.numpy as jnp
import numpy as np
from jax import lax
from jax.experimental import pallas as pl
from jax.experimental.pallas import tpu as pltpu
from jax.sharding import PartitionSpec as P

BLOCK = 16
TILE = 128
BAND = 9
TILE_DEV = 8
HALF = BAND // 2
NB = TILE // BLOCK
WIN = TILE_DEV + 2 * HALF
NT = TILE_DEV * BAND
LANES = 128
CODE_LANE = 112
MESH = pl.DeviceIdType.MESH
f32 = jnp.float32
bf16 = jnp.bfloat16


def split2(x):
    hi = x.astype(bf16)
    return hi, (x - hi.astype(f32)).astype(bf16)


def mm(a, b):
    return jnp.dot(a, b, preferred_element_type=f32)


def piece_columns(groups, cols):
    per = BLOCK * cols
    sub = cols * cols
    perm = np.zeros((BLOCK * BLOCK, groups * LANES), np.float32)
    for g in range(groups):
        for k in range(per):
            perm[g * per + k, g * LANES + k] = 1
        at = g * LANES + per
        for other in range(groups):
            if other != g:
                for k in range(sub):
                    perm[other * per + g * sub + k, at + k] = 1
                at += sub
    return perm


def spread_columns(groups, cols):
    per = BLOCK * cols
    sub = cols * cols
    width = TILE // groups
    by_col = np.zeros((LANES, cols * TILE), np.float32)
    by_row = np.zeros((groups, LANES, cols * TILE), np.float32)
    for u in range(cols):
        for lane in range(TILE):
            comp = lane // width * cols + lane % cols
            by_col[comp * cols + u, u * TILE + lane] = 1
            for g in range(groups):
                other = lane // width
                if other == g:
                    k = (g * cols + u) * cols + lane % cols
                else:
                    k = per + (other - (other > g)) * sub + u * cols + lane % cols
                by_row[g, k, u * TILE + lane] = 1
    return by_col, by_row


def route_kernel(rows, cap, groups, feats, owner_row, code_col, w1, w2, w3, perm, out):
    edges = feats.shape[0]
    h1 = mm(feats[...], w1[...])
    h1 = (h1 / (1.0 + jnp.exp(-h1))).astype(bf16)
    h2 = mm(h1, w2[...])
    h2 = (h2 / (1.0 + jnp.exp(-h2))).astype(bf16)
    w3p = mm(w3[...], perm[...]).astype(bf16)
    vals = mm(h2, w3p)
    lane = lax.broadcasted_iota(jnp.int32, vals.shape, 1)
    vals = jnp.where(lane % LANES == CODE_LANE, code_col[...].astype(f32), vals)
    owner = owner_row[...]
    names = (owner == lax.broadcasted_iota(jnp.int32, (rows, edges), 0)).astype(f32)
    before = (
        lax.broadcasted_iota(jnp.int32, (edges, edges), 0)
        < lax.broadcasted_iota(jnp.int32, (edges, edges), 1)
    ).astype(bf16)
    rank = jnp.sum(names * mm(names.astype(bf16), before), axis=0, keepdims=True).astype(jnp.int32)
    target = owner * cap + rank
    place = (target == lax.broadcasted_iota(jnp.int32, (rows * cap, edges), 0)).astype(bf16)
    hi, lo = split2(vals)
    sent = mm(place, hi) + mm(place, lo)
    for g in range(groups):
        part = sent[:, g * LANES : (g + 1) * LANES]
        out[:, g] = part.reshape(rows, cap, LANES)


def own_tiles():
    return [(i, j) for i in range(TILE_DEV) for j in range(TILE_DEV) if abs(i - j) <= HALF]


def tile_at(i, j):
    return i * BAND + j - i + HALF


LOW = [(a, b) for a in range(HALF) for b in range(HALF)]
LOW_PART = [(j, i) for j in range(HALF) for i in range(j - HALF, 0)]
HIGH_PART = [
    (j, i) for j in range(TILE_DEV - HALF, TILE_DEV) for i in range(TILE_DEV, j + HALF + 1)
]
CORNER = len(LOW)
E_HALO = CORNER + len(LOW_PART)


def band_kernel(
    rows, groups, scale,
    rec, by_col, by_row, out,
    dh, rh, ge, gw, se, re, sw, rw, bhi, blo, ahi, alo, t0, t1, s_sem, r_sem,
):
    r = lax.axis_index("rows")
    g = lax.axis_index("feat")
    width = TILE // groups
    cols = BLOCK // groups
    up, down = lax.rem(r + 1, rows), lax.rem(r + rows - 1, rows)
    y, c = g // 2, g % 2
    by_slot = [g, y * 2 + (1 - c), (1 - y) * 2 + c, (1 - y) * 2 + (1 - c)]
    core_peer, y_peer = by_slot[1], by_slot[2]

    barrier = pltpu.get_barrier_semaphore()
    for who in ((up, g), (down, g), (r, core_peer), (r, y_peer)):
        pl.semaphore_signal(barrier, inc=1, device_id=who, device_id_type=MESH)
    pl.semaphore_wait(barrier, 4)

    x = rec[...]
    count = x.shape[0]
    code_c = x[:, CODE_LANE : CODE_LANE + 1].astype(jnp.int32)
    code_r = x.T[CODE_LANE : CODE_LANE + 1, :].astype(jnp.int32)
    hi, lo = split2(x)
    lane = lax.broadcasted_iota(jnp.int32, (count, cols * TILE), 1)
    lane_block = lane % width // cols
    tile_id = lax.shift_right_logical(code_r, 10) % 8 * BAND + lax.shift_right_logical(code_r, 3) % 16
    valid = code_r >= 8192
    src_r, dst_r = lax.shift_right_logical(code_r, 7) % 8, code_r % 8
    src_c, dst_c = lax.shift_right_logical(code_c, 7) % 8, code_c % 8
    line = lax.broadcasted_iota(jnp.int32, (NT * NB, count), 0)
    for dest, spread, row_block, lane_of in (
        (dh, by_col, dst_r, src_c),
        (rh, by_row, src_r, dst_c),
    ):
        index = jnp.where(valid, tile_id * NB + row_block, -1)
        place = (line == index).astype(bf16)
        keep = lane_block == lane_of
        strips_hi = jnp.where(keep, mm(hi, spread[...]), 0.0).astype(bf16)
        strips_lo = jnp.where(keep, mm(lo, spread[...]), 0.0).astype(bf16)
        total = mm(place, strips_hi) + mm(place, strips_lo)
        for u in range(cols):
            dest[:, pl.ds(u, NB, stride=cols), :] = total[:, u * TILE : (u + 1) * TILE].reshape(
                NT, NB, TILE
            )

    zero_block = jnp.zeros((TILE, TILE), bf16)
    for p in range(TILE_DEV // 2):
        for i, kk in ((2 * p, 2 * p + 9), (2 * p + 1, 2 * p)):
            for ref in (bhi, blo):
                ref[kk * TILE : (kk + 1) * TILE, i * TILE : (i + 1) * TILE] = zero_block
    ahi[...] = jnp.zeros(ahi.shape, bf16)
    alo[...] = jnp.zeros(alo.shape, bf16)

    def copy(src, dst, sem, who):
        return pltpu.make_async_remote_copy(
            src_ref=src, dst_ref=dst, send_sem=s_sem.at[sem], recv_sem=r_sem.at[sem],
            device_id=who, device_id_type=MESH,
        )

    def gather(buf, base):
        near = copy(buf.at[0], buf.at[1], base, (r, core_peer))
        far = copy(buf.at[0], buf.at[2], base + 1, (r, y_peer))
        near.start()
        far.start()
        far.wait_recv()
        on = copy(buf.at[2], buf.at[3], base + 2, (r, core_peer))
        on.start()
        near.wait_recv()
        on.wait_recv()
        return [near, far, on]

    def pack_corners(send, buf):
        for n, (a, b) in enumerate(LOW):
            send[0, n] = buf[0, tile_at(a, b)]
            send[1, n] = buf[0, tile_at(a + HALF, b + HALF)]

    def exchange(send, recv, base):
        to_low = copy(send.at[0], recv.at[1], base, (down, g))
        to_high = copy(send.at[1], recv.at[0], base + 1, (up, g))
        to_low.start()
        to_high.start()
        return [to_low, to_high]

    def put_a(jj, kk, val):
        h, l = split2(val)
        ahi[jj * width : (jj + 1) * width, kk * TILE : (kk + 1) * TILE] = h
        alo[jj * width : (jj + 1) * width, kk * TILE : (kk + 1) * TILE] = l

    halo_tiles = [
        (j, kk) for j in range(TILE_DEV) for kk in list(range(HALF)) + list(range(WIN - HALF, WIN))
        if 0 <= kk - j < BAND
    ]

    def build(buf, halos):
        for i in range(TILE_DEV):
            for s in range(BAND):
                for slot in range(4):
                    h, l = split2(buf[slot, i * BAND + s])
                    at = pl.multiple_of((i + s) * TILE + by_slot[slot] * width, width)
                    bhi[pl.ds(at, width), i * TILE : (i + 1) * TILE] = h
                    blo[pl.ds(at, width), i * TILE : (i + 1) * TILE] = l
                put_a(i + s, i + HALF, buf[0, i * BAND + s])
        for n, (a, b) in enumerate(LOW):
            put_a(b, a, halos[0, n])
            put_a(b + WIN - HALF, a + WIN - HALF, halos[1, n])
        for n, (j, kk) in enumerate(halo_tiles):
            for slot in range(4):
                at = pl.multiple_of(by_slot[slot] * width, width)
                t0[n, pl.ds(at, width), :] = buf[slot, j * BAND + kk - j]
        for n, (j, kk) in enumerate(halo_tiles):
            t1[n] = t0[n].T
        for n, (j, kk) in enumerate(halo_tiles):
            put_a(j + HALF, kk, t1[n, pl.ds(pl.multiple_of(g * width, width), width), :])

    def product(emit):
        for p in range(TILE_DEV // 2):
            rows_at = slice(2 * p * width, (2 * p + 10) * width)
            mid = slice(2 * p * TILE, (2 * p + 10) * TILE)
            cols_at = slice(2 * p * TILE, (2 * p + 2) * TILE)
            a_h, b_h = ahi[rows_at, mid], bhi[mid, cols_at]
            acc = mm(a_h, b_h) + mm(a_h, blo[mid, cols_at]) + mm(alo[rows_at, mid], b_h)
            for di in range(2):
                for s in range(BAND):
                    m = s + di
                    emit(2 * p + di, s, acc[m * width : (m + 1) * width, di * TILE : (di + 1) * TILE])

    for i, j in own_tiles():
        ge[0, tile_at(i, j)] = scale * (dh[tile_at(i, j)] + rh[tile_at(j, i)])
    pack_corners(se, ge)
    for n, (j, i) in enumerate(LOW_PART):
        se[0, CORNER + n] = rh[tile_at(j, i)]
    for n, (j, i) in enumerate(HIGH_PART):
        se[1, CORNER + n] = rh[tile_at(j, i)]
    pending = exchange(se, re, 0)
    for item in pending:
        item.wait_recv()
    for n, (j, i) in enumerate(HIGH_PART):
        own, halo = i - TILE_DEV, j - TILE_DEV
        ge[0, tile_at(own, halo)] = scale * (dh[tile_at(own, halo)] + re[0, CORNER + n])
    for n, (j, i) in enumerate(LOW_PART):
        own, halo = i + TILE_DEV, j + TILE_DEV
        ge[0, tile_at(own, halo)] = scale * (dh[tile_at(own, halo)] + re[1, CORNER + n])
    pending += gather(ge, 2)
    build(ge, re)

    def first(i, s, acc):
        gw[0, i * BAND + s] = ge[0, i * BAND + s] + acc

    product(first)
    pack_corners(sw, gw)
    more = exchange(sw, rw, 5)
    pending += more
    pending += gather(gw, 7)
    for item in more:
        item.wait_recv()
    build(gw, rw)
    eye = (
        lax.broadcasted_iota(jnp.int32, (width, TILE), 0) + g * width
        == lax.broadcasted_iota(jnp.int32, (width, TILE), 1)
    ).astype(f32)

    def second(i, s, acc):
        val = 1.5 * gw[0, i * BAND + s] - acc
        if s == HALF:
            val = val + 0.4375 * eye
        out[i, s] = val

    product(second)
    for item in pending:
        item.wait_send()


def local(edge_feats, edge_owner, src_local, band_slot, dst_local, w_first, w_second, w_third):
    groups = lax.axis_size("feat")
    rows = lax.axis_size("rows")
    edges = edge_feats.shape[0]
    cap = max(2, 2 * edges // rows)
    cols = BLOCK // groups
    width = TILE // groups
    code = 8192 + src_local * 128 + band_slot * 8 + dst_local
    vm = pl.BlockSpec(memory_space=pltpu.VMEM)
    perm = jnp.asarray(piece_columns(groups, cols), bf16)
    by_col, by_row = spread_columns(groups, cols)
    by_col = jnp.asarray(by_col, bf16)
    by_row = jnp.asarray(by_row, bf16)[lax.axis_index("feat")]
    sent = pl.pallas_call(
        functools.partial(route_kernel, rows, cap, groups),
        out_shape=jax.ShapeDtypeStruct((rows, groups, cap, LANES), f32),
        in_specs=[vm] * 7,
        out_specs=vm,
        compiler_params=pltpu.CompilerParams(vmem_limit_bytes=32 << 20),
    )(edge_feats, edge_owner.reshape(1, edges), code.reshape(edges, 1), w_first, w_second, w_third, perm)
    sent = sent.reshape(rows * groups, cap, LANES)
    got = lax.all_to_all(sent, ("rows", "feat"), 0, 0, tiled=True)
    rec = got.reshape(rows * groups * cap, LANES)
    degree = groups * edges / (TILE_DEV * NB)
    scale = 0.5 * (0.5 / math.sqrt(2.0 * BLOCK * degree))
    tiles = (NT, width, TILE)
    return pl.pallas_call(
        functools.partial(band_kernel, rows, groups, scale),
        out_shape=jax.ShapeDtypeStruct((TILE_DEV, BAND, width, TILE), f32),
        in_specs=[vm] * 3,
        out_specs=vm,
        scratch_shapes=[
            pltpu.VMEM(tiles, f32),
            pltpu.VMEM(tiles, f32),
            pltpu.VMEM((4,) + tiles, f32),
            pltpu.VMEM((4,) + tiles, f32),
            pltpu.VMEM((2, E_HALO, width, TILE), f32),
            pltpu.VMEM((2, E_HALO, width, TILE), f32),
            pltpu.VMEM((2, CORNER, width, TILE), f32),
            pltpu.VMEM((2, CORNER, width, TILE), f32),
            pltpu.VMEM((WIN * TILE, TILE_DEV * TILE), bf16),
            pltpu.VMEM((WIN * TILE, TILE_DEV * TILE), bf16),
            pltpu.VMEM((WIN * width, WIN * TILE), bf16),
            pltpu.VMEM((WIN * width, WIN * TILE), bf16),
            pltpu.VMEM((20, TILE, TILE), f32),
            pltpu.VMEM((20, TILE, TILE), f32),
            pltpu.SemaphoreType.DMA((10,)),
            pltpu.SemaphoreType.DMA((10,)),
        ],
        compiler_params=pltpu.CompilerParams(
            collective_id=0, has_side_effects=True, vmem_limit_bytes=60 << 20
        ),
    )(rec, by_col, by_row)


def solution(mesh):
    in_specs = (
        P(("rows", "feat"), None),
        P(("rows", "feat"), None),
        P(("rows", "feat")),
        P(("rows", "feat")),
        P(("rows", "feat")),
        P(),
        P(),
        P(),
    )
    out_specs = P("rows", None, "feat", None)
    return jax.shard_map(local, mesh=mesh, in_specs=in_specs, out_specs=out_specs, check_vma=False)
```

```python
import functools
import math

import jax
import jax.numpy as jnp
from jax import lax
from jax.experimental import pallas as pl
from jax.experimental.pallas import tpu as pltpu
from jax.sharding import PartitionSpec as P

BLOCK = 16
TILE = 128
BAND = 9
TILE_DEV = 8
HALF = BAND // 2
NB = TILE // BLOCK
WIN = TILE_DEV + 2 * HALF
NT = TILE_DEV * BAND
LANES = 128
CODE_LANE = 112
MESH = pl.DeviceIdType.MESH
f32 = jnp.float32
bf16 = jnp.bfloat16


def split2(x):
    hi = x.astype(bf16)
    return hi, (x - hi.astype(f32)).astype(bf16)


def mm(a, b):
    return jnp.dot(a, b, preferred_element_type=f32)


def piece_columns(groups, cols):
    per = BLOCK * cols
    sub = cols * cols
    shape = (BLOCK * BLOCK, groups * LANES)
    source = lax.broadcasted_iota(jnp.int32, shape, 0)
    lane = lax.broadcasted_iota(jnp.int32, shape, 1)
    g, k = lane // LANES, lane % LANES
    other = (k - per) // sub
    other = other + (other >= g).astype(jnp.int32)
    from_row = other * per + g * sub + (k - per) % sub
    want = jnp.where(k < per, g * per + k, jnp.where(k < CODE_LANE, from_row, -1))
    return (source == want).astype(bf16)


def spread_columns(groups, cols, g):
    per = BLOCK * cols
    sub = cols * cols
    width = TILE // groups
    shape = (LANES, cols * TILE)
    source = lax.broadcasted_iota(jnp.int32, shape, 0)
    full = lax.broadcasted_iota(jnp.int32, shape, 1)
    u, lane = full // TILE, full % TILE
    other, unit = lane // width, lane % cols
    by_col = source == (other * cols + unit) * cols + u
    apart = per + (other - (other > g).astype(jnp.int32)) * sub + u * cols + unit
    by_row = source == jnp.where(other == g, (g * cols + u) * cols + unit, apart)
    return by_col.astype(bf16), by_row.astype(bf16)


def route_kernel(
    rows, cap, groups, feats_in, owner_in, code_in, w1_in, w2_in, w3_in, out,
    feats, owner_row, code_col, w1, w2, w3, sems,
):
    fetches = []
    for n, (src, dst) in enumerate(
        ((feats_in, feats), (w1_in, w1), (w2_in, w2), (w3_in, w3), (owner_in, owner_row), (code_in, code_col))
    ):
        fetch = pltpu.make_async_copy(src, dst, sems.at[n])
        fetch.start()
        fetches.append(fetch)
    edges = feats.shape[0]
    perm = piece_columns(groups, BLOCK // groups)
    before = (
        lax.broadcasted_iota(jnp.int32, (edges, edges), 0)
        < lax.broadcasted_iota(jnp.int32, (edges, edges), 1)
    ).astype(bf16)
    for fetch in fetches:
        fetch.wait()
    h1 = mm(feats[...], w1[...])
    h1 = (h1 / (1.0 + jnp.exp(-h1))).astype(bf16)
    h2 = mm(h1, w2[...])
    h2 = (h2 / (1.0 + jnp.exp(-h2))).astype(bf16)
    w3p = mm(w3[...], perm).astype(bf16)
    vals = mm(h2, w3p)
    lane = lax.broadcasted_iota(jnp.int32, vals.shape, 1)
    vals = jnp.where(lane % LANES == CODE_LANE, code_col[...].astype(f32), vals)
    owner = owner_row[...]
    names = (owner == lax.broadcasted_iota(jnp.int32, (rows, edges), 0)).astype(f32)
    rank = jnp.sum(names * mm(names.astype(bf16), before), axis=0, keepdims=True).astype(jnp.int32)
    target = owner * cap + rank
    place = (target == lax.broadcasted_iota(jnp.int32, (rows * cap, edges), 0)).astype(bf16)
    hi, lo = split2(vals)
    sent = mm(place, hi) + mm(place, lo)
    for g in range(groups):
        part = sent[:, g * LANES : (g + 1) * LANES]
        out[:, g] = part.reshape(rows, cap, LANES)


def own_tiles():
    return [(i, j) for i in range(TILE_DEV) for j in range(TILE_DEV) if abs(i - j) <= HALF]


def tile_at(i, j):
    return i * BAND + j - i + HALF


LOW = [(a, b) for a in range(HALF) for b in range(HALF)]
LOW_PART = [(j, i) for j in range(HALF) for i in range(j - HALF, 0)]
HIGH_PART = [
    (j, i) for j in range(TILE_DEV - HALF, TILE_DEV) for i in range(TILE_DEV, j + HALF + 1)
]
CORNER = len(LOW)
PART = len(LOW_PART)
PAIRS = TILE_DEV // 2


def halo_of(i):
    return [j for j in range(i - HALF, i + HALF + 1) if not 0 <= j < TILE_DEV]


E_CHUNKS = [
    [t for t in own_tiles() if t[0] <= t[1]],
    [(i, j) for i in range(TILE_DEV) for j in halo_of(i)],
]
W_CHUNKS = [
    [
        (i, j)
        for i in (2 * p, 2 * p + 1)
        for j in range(i - HALF, i + HALF + 1)
        if not (0 <= j < i)
    ]
    for p in range(PAIRS)
]
E_AT = {t: n for n, t in enumerate(sum(E_CHUNKS, []))}
W_AT = {t: n for n, t in enumerate(sum(W_CHUNKS, []))}
SENT = len(E_AT)
HALO_SLOT = {t: n for n, t in enumerate(E_CHUNKS[1])}


def band_kernel(
    rows, groups, scale, rec, out,
    dh, rh, le, lw, fe, fw, sp, rp, se, re, sw, rw, bhi, blo, ahi, alo, t1, s_sem, r_sem,
):
    r = lax.axis_index("rows")
    g = lax.axis_index("feat")
    width = TILE // groups
    cols = BLOCK // groups
    up, down = lax.rem(r + 1, rows), lax.rem(r + rows - 1, rows)
    y, c = g // 2, g % 2
    core_peer, y_peer = y * 2 + (1 - c), (1 - y) * 2 + c
    mine = pl.ds(pl.multiple_of(g * width, width), width)
    theirs = pl.ds(pl.multiple_of(y_peer * width, width), width)

    barrier = pltpu.get_barrier_semaphore()
    for who in ((up, g), (down, g), (r, core_peer), (r, y_peer)):
        pl.semaphore_signal(barrier, inc=1, device_id=who, device_id_type=MESH)

    x = rec[...]
    count = x.shape[0]
    code_c = x[:, CODE_LANE : CODE_LANE + 1].astype(jnp.int32)
    code_r = x.T[CODE_LANE : CODE_LANE + 1, :].astype(jnp.int32)
    hi, lo = split2(x)
    lane = lax.broadcasted_iota(jnp.int32, (1, cols * TILE), 1)
    lane_block = lane % width // cols
    tile_id = lax.shift_right_logical(code_r, 10) % 8 * BAND + lax.shift_right_logical(code_r, 3) % 16
    valid = code_r >= 8192
    src_r, dst_r = lax.shift_right_logical(code_r, 7) % 8, code_r % 8
    src_c, dst_c = lax.shift_right_logical(code_c, 7) % 8, code_c % 8
    line = lax.broadcasted_iota(jnp.int32, (NT * NB, count), 0)
    by_col, by_row = spread_columns(groups, cols, g)

    def scatter(dest, spread, row_block, lane_of):
        index = jnp.where(valid, tile_id * NB + row_block, -1)
        place = (line == index).astype(bf16)
        keep = lane_block == lane_of
        strips_hi = jnp.where(keep, mm(hi, spread), 0.0).astype(bf16)
        strips_lo = jnp.where(keep, mm(lo, spread), 0.0).astype(bf16)
        total = mm(place, strips_hi) + mm(place, strips_lo)
        for u in range(cols):
            dest[:, pl.ds(u, NB, stride=cols), :] = total[:, u * TILE : (u + 1) * TILE].reshape(
                NT, NB, TILE
            )

    def copy(src, dst, sem, who):
        return pltpu.make_async_remote_copy(
            src_ref=src, dst_ref=dst, send_sem=s_sem.at[sem], recv_sem=r_sem.at[sem],
            device_id=who, device_id_type=MESH,
        )

    pending = []

    def start(*args):
        item = copy(*args)
        item.start()
        pending.append(item)
        return item

    def gather(buf, first, size, sem):
        part = buf.at[pl.ds(first, size), mine]
        near = start(part, part, sem, (r, core_peer))
        far = start(part, part, sem + 1, (r, y_peer))
        return near, far, buf.at[pl.ds(first, size), theirs], sem + 2

    def forward(item):
        item[1].wait_recv()
        return start(item[2], item[2], item[3], (r, core_peer))

    def put_a(jj, kk, val):
        h, l = split2(val)
        ahi[jj * width : (jj + 1) * width, kk * TILE : (kk + 1) * TILE] = h
        alo[jj * width : (jj + 1) * width, kk * TILE : (kk + 1) * TILE] = l

    def put_b(kk, i, val):
        h, l = split2(val)
        bhi[kk * TILE : (kk + 1) * TILE, i * TILE : (i + 1) * TILE] = h
        blo[kk * TILE : (kk + 1) * TILE, i * TILE : (i + 1) * TILE] = l

    def build_own(buf, rows_of):
        for i in rows_of:
            for s in range(BAND):
                put_a(i + s, i + HALF, buf[i * BAND + s])

    def build_corner(recv, side):
        at = 0 if side == 0 else WIN - HALF
        for n, (a, b) in enumerate(LOW):
            put_a(b + at, a + at, recv[side, n])

    def build_tiles(buf, index, tiles):
        for i, j in tiles:
            full = buf[index[i, j]]
            put_b(j + HALF, i, full)
            if i != j:
                turned = full.T
                if 0 <= j < TILE_DEV:
                    put_b(i + HALF, j, turned)
                else:
                    t1[HALO_SLOT[i, j]] = turned
        for i, j in tiles:
            if not 0 <= j < TILE_DEV:
                put_a(i + HALF, j + HALF, t1[HALO_SLOT[i, j], mine, :])

    def product(p, emit):
        rows_at = slice(2 * p * width, (2 * p + 10) * width)
        mid = slice(2 * p * TILE, (2 * p + 10) * TILE)
        cols_at = slice(2 * p * TILE, (2 * p + 2) * TILE)
        a_h, b_h = ahi[rows_at, mid], bhi[mid, cols_at]
        acc = mm(a_h, b_h) + mm(a_h, blo[mid, cols_at]) + mm(alo[rows_at, mid], b_h)
        for di in range(2):
            for s in range(BAND):
                m = s + di
                emit(2 * p + di, s, acc[m * width : (m + 1) * width, di * TILE : (di + 1) * TILE])

    scatter(rh, by_row, src_r, dst_c)
    for n, (j, i) in enumerate(LOW_PART):
        sp[0, n] = rh[tile_at(j, i)]
    for n, (j, i) in enumerate(HIGH_PART):
        sp[1, n] = rh[tile_at(j, i)]
    pl.semaphore_wait(barrier, 4)
    part_low = start(sp.at[0], rp.at[1], 0, (down, g))
    part_high = start(sp.at[1], rp.at[0], 1, (up, g))
    scatter(dh, by_col, dst_r, src_c)
    for i, j in own_tiles():
        val = scale * (dh[tile_at(i, j)] + rh[tile_at(j, i)])
        le[tile_at(i, j)] = val
        if i <= j:
            fe[E_AT[i, j], mine, :] = val
    first_chunk = gather(fe, 0, len(E_CHUNKS[0]), 2)
    for n, (a, b) in enumerate(LOW):
        se[0, n] = le[tile_at(a, b)]
        se[1, n] = le[tile_at(a + HALF, b + HALF)]
    part_low.wait_recv()
    part_high.wait_recv()
    for n, (j, i) in enumerate(HIGH_PART):
        own, halo = i - TILE_DEV, j - TILE_DEV
        val = scale * (dh[tile_at(own, halo)] + rp[0, n])
        le[tile_at(own, halo)] = val
        fe[E_AT[own, halo], mine, :] = val
    for n, (j, i) in enumerate(LOW_PART):
        own, halo = i + TILE_DEV, j + TILE_DEV
        val = scale * (dh[tile_at(own, halo)] + rp[1, n])
        le[tile_at(own, halo)] = val
        fe[E_AT[own, halo], mine, :] = val
    second_chunk = gather(fe, len(E_CHUNKS[0]), len(E_CHUNKS[1]), 5)
    to_low = start(se.at[0], re.at[1], 8, (down, g))
    to_high = start(se.at[1], re.at[0], 9, (up, g))

    zero_block = jnp.zeros((TILE, TILE), bf16)
    for p in range(PAIRS):
        for i, kk in ((2 * p, 2 * p + 9), (2 * p + 1, 2 * p)):
            for ref in (bhi, blo):
                ref[kk * TILE : (kk + 1) * TILE, i * TILE : (i + 1) * TILE] = zero_block
    ahi[...] = jnp.zeros(ahi.shape, bf16)
    alo[...] = jnp.zeros(alo.shape, bf16)
    build_own(le, range(TILE_DEV))
    on = forward(first_chunk)
    first_chunk[0].wait_recv()
    on.wait_recv()
    build_tiles(fe, E_AT, E_CHUNKS[0])
    on = forward(second_chunk)
    second_chunk[0].wait_recv()
    on.wait_recv()
    build_tiles(fe, E_AT, E_CHUNKS[1])
    to_low.wait_recv()
    to_high.wait_recv()
    for side in range(2):
        build_corner(re, side)

    def first(i, s, acc):
        val = le[i * BAND + s] + acc
        lw[i * BAND + s] = val
        if (i, i + s - HALF) in W_AT:
            fw[W_AT[i, i + s - HALF], mine, :] = val

    chunks = []
    begin = 0
    corners = [None, None]
    for p in range(PAIRS):
        product(p, first)
        chunks.append(gather(fw, begin, len(W_CHUNKS[p]), 10 + 3 * p))
        begin += len(W_CHUNKS[p])
        if p == PAIRS // 2 - 1:
            for n, (a, b) in enumerate(LOW):
                sw[0, n] = lw[tile_at(a, b)]
            corners[1] = start(sw.at[0], rw.at[1], 22, (down, g))
    for n, (a, b) in enumerate(LOW):
        sw[1, n] = lw[tile_at(a + HALF, b + HALF)]
    corners[0] = start(sw.at[1], rw.at[0], 23, (up, g))
    build_own(lw, range(TILE_DEV))
    eye = (
        lax.broadcasted_iota(jnp.int32, (width, TILE), 0) + g * width
        == lax.broadcasted_iota(jnp.int32, (width, TILE), 1)
    ).astype(f32)

    def second(i, s, acc):
        val = 1.5 * lw[i * BAND + s] - acc
        if s == HALF:
            val = val + 0.4375 * eye
        out[i, s] = val

    for half in range(2):
        for p in (2 * half, 2 * half + 1):
            on = forward(chunks[p])
            chunks[p][0].wait_recv()
            on.wait_recv()
            build_tiles(fw, W_AT, W_CHUNKS[p])
        corners[half].wait_recv()
        build_corner(rw, half)
        for p in (2 * half, 2 * half + 1):
            product(p, second)
    for item in pending:
        item.wait_send()


def local(edge_feats, edge_owner, src_local, band_slot, dst_local, w_first, w_second, w_third):
    groups = lax.axis_size("feat")
    rows = lax.axis_size("rows")
    edges = edge_feats.shape[0]
    cap = max(2, 2 * edges // rows)
    width = TILE // groups
    code = 8192 + src_local * 128 + band_slot * 8 + dst_local
    vm = pl.BlockSpec(memory_space=pltpu.VMEM)
    operands = (
        edge_feats, edge_owner.reshape(1, edges), code.reshape(edges, 1), w_first, w_second, w_third,
    )
    sent = pl.pallas_call(
        functools.partial(route_kernel, rows, cap, groups),
        out_shape=jax.ShapeDtypeStruct((rows, groups, cap, LANES), f32),
        in_specs=[pl.BlockSpec(memory_space=pl.ANY)] * 6,
        out_specs=vm,
        scratch_shapes=[pltpu.VMEM(item.shape, item.dtype) for item in operands]
        + [pltpu.SemaphoreType.DMA((6,))],
        compiler_params=pltpu.CompilerParams(vmem_limit_bytes=56 << 20),
    )(*operands)
    sent = sent.reshape(rows * groups, cap, LANES)
    got = lax.all_to_all(sent, ("rows", "feat"), 0, 0, tiled=True)
    rec = got.reshape(rows * groups * cap, LANES)
    degree = groups * edges / (TILE_DEV * NB)
    scale = 0.5 * (0.5 / math.sqrt(2.0 * BLOCK * degree))
    tiles = (NT, width, TILE)
    return pl.pallas_call(
        functools.partial(band_kernel, rows, groups, scale),
        out_shape=jax.ShapeDtypeStruct((TILE_DEV, BAND, width, TILE), f32),
        in_specs=[vm],
        out_specs=vm,
        scratch_shapes=[pltpu.VMEM(tiles, f32)] * 4
        + [pltpu.VMEM((SENT, TILE, TILE), f32)] * 2
        + [pltpu.VMEM((2, PART, width, TILE), f32)] * 2
        + [pltpu.VMEM((2, CORNER, width, TILE), f32)] * 4
        + [pltpu.VMEM((WIN * TILE, TILE_DEV * TILE), bf16)] * 2
        + [pltpu.VMEM((WIN * width, WIN * TILE), bf16)] * 2
        + [pltpu.VMEM((len(HALO_SLOT), TILE, TILE), f32)]
        + [pltpu.SemaphoreType.DMA((24,))] * 2,
        compiler_params=pltpu.CompilerParams(
            collective_id=0, has_side_effects=True, vmem_limit_bytes=60 << 20
        ),
    )(rec)


def solution(mesh):
    in_specs = (
        P(("rows", "feat"), None),
        P(("rows", "feat"), None),
        P(("rows", "feat")),
        P(("rows", "feat")),
        P(("rows", "feat")),
        P(),
        P(),
        P(),
    )
    out_specs = P("rows", None, "feat", None)
    return jax.shard_map(local, mesh=mesh, in_specs=in_specs, out_specs=out_specs, check_vma=False)
```

```python
import functools
import math

import jax
import jax.numpy as jnp
from jax import lax
from jax.experimental import pallas as pl
from jax.experimental.pallas import tpu as pltpu
from jax.sharding import PartitionSpec as P

BLOCK = 16
TILE = 128
BAND = 9
TILE_DEV = 8
HALF = BAND // 2
NB = TILE // BLOCK
WIN = TILE_DEV + 2 * HALF
NT = TILE_DEV * BAND
LANES = 128
CODE_LANE = 112
MESH = pl.DeviceIdType.MESH
f32 = jnp.float32
bf16 = jnp.bfloat16


def split2(x):
    hi = x.astype(bf16)
    return hi, (x - hi.astype(f32)).astype(bf16)


def mm(a, b):
    return jnp.dot(a, b, preferred_element_type=f32)


def piece_columns(groups, cols):
    per = BLOCK * cols
    sub = cols * cols
    shape = (BLOCK * BLOCK, groups * LANES)
    source = lax.broadcasted_iota(jnp.int32, shape, 0)
    lane = lax.broadcasted_iota(jnp.int32, shape, 1)
    g, k = lane // LANES, lane % LANES
    other = (k - per) // sub
    other = other + (other >= g).astype(jnp.int32)
    from_row = other * per + g * sub + (k - per) % sub
    want = jnp.where(k < per, g * per + k, jnp.where(k < CODE_LANE, from_row, -1))
    return (source == want).astype(bf16)


def spread_columns(groups, cols, g):
    per = BLOCK * cols
    sub = cols * cols
    width = TILE // groups
    shape = (LANES, cols * TILE)
    source = lax.broadcasted_iota(jnp.int32, shape, 0)
    full = lax.broadcasted_iota(jnp.int32, shape, 1)
    u, lane = full // TILE, full % TILE
    other, unit = lane // width, lane % cols
    by_col = source == (other * cols + unit) * cols + u
    apart = per + (other - (other > g).astype(jnp.int32)) * sub + u * cols + unit
    by_row = source == jnp.where(other == g, (g * cols + u) * cols + unit, apart)
    return by_col.astype(bf16), by_row.astype(bf16)


def route_kernel(
    rows, cap, groups,
    feats_in, owner_in, src_in, slot_in, dst_in, w1_in, w2_in, w3_in, dh, rh,
    feats, owner_row, src_row, slot_row, dst_row, w1, w2, w3, sent, rec, acc_col, acc_row,
    sems, s_sem, r_sem,
):
    r = lax.axis_index("rows")
    g = lax.axis_index("feat")
    n = rows * groups
    edges = feats.shape[0]
    cols = BLOCK // groups
    width = TILE // groups

    def partner(q):
        turn = q // groups
        step = rows // 2 + (turn + 1) // 2 * (1 - 2 * (turn % 2))
        return (r + step + rows) % rows, (g + groups - 1 - q % groups) % groups

    def record_copy(q):
        to_row, to_group = partner(q)
        return pltpu.make_async_remote_copy(
            src_ref=sent.at[to_row, to_group], dst_ref=rec.at[q],
            send_sem=s_sem.at[q], recv_sem=r_sem.at[q],
            device_id=(to_row, to_group), device_id_type=MESH,
        )

    barrier = pltpu.get_barrier_semaphore()

    def greet(q, carry):
        pl.semaphore_signal(barrier, inc=1, device_id=partner(q), device_id_type=MESH)
        return carry

    lax.fori_loop(0, n - 1, greet, 0)

    fetches = []
    for k, (src, dst) in enumerate(
        (
            (feats_in, feats), (w1_in, w1), (w2_in, w2), (w3_in, w3), (owner_in, owner_row),
            (src_in, src_row), (slot_in, slot_row), (dst_in, dst_row),
        )
    ):
        fetch = pltpu.make_async_copy(src, dst, sems.at[k])
        fetch.start()
        fetches.append(fetch)
    perm = piece_columns(groups, cols)
    before = (
        lax.broadcasted_iota(jnp.int32, (edges, edges), 0)
        < lax.broadcasted_iota(jnp.int32, (edges, edges), 1)
    ).astype(bf16)
    for fetch in fetches:
        fetch.wait()
    h1 = mm(feats[...], w1[...])
    h1 = (h1 / (1.0 + jnp.exp(-h1))).astype(bf16)
    h2 = mm(h1, w2[...])
    h2 = (h2 / (1.0 + jnp.exp(-h2))).astype(bf16)
    w3p = mm(w3[...], perm).astype(bf16)
    vals = mm(h2, w3p)
    code = (8192 + src_row[...] * 128 + slot_row[...] * 8 + dst_row[...]).astype(f32)
    code_col = jnp.broadcast_to(code, (LANES, edges)).T[:, :1]
    lane = lax.broadcasted_iota(jnp.int32, vals.shape, 1)
    vals = jnp.where(lane % LANES == CODE_LANE, code_col, vals)
    owner = owner_row[...]
    names = (owner == lax.broadcasted_iota(jnp.int32, (rows, edges), 0)).astype(f32)
    rank = jnp.sum(names * mm(names.astype(bf16), before), axis=0, keepdims=True).astype(jnp.int32)
    target = owner * cap + rank
    place = (target == lax.broadcasted_iota(jnp.int32, (rows * cap, edges), 0)).astype(bf16)
    hi, lo = split2(vals)
    packed = mm(place, hi) + mm(place, lo)
    for k in range(groups):
        part = packed[:, k * LANES : (k + 1) * LANES]
        sent[:, k] = part.reshape(rows, cap, LANES)

    pl.semaphore_wait(barrier, n - 1)

    def send(q, carry):
        record_copy(q).start()
        return carry

    lax.fori_loop(0, n - 1, send, 0)
    rec[n - 1] = sent[r, g]

    by_col, by_row = spread_columns(groups, cols, g)
    spread_lane = lax.broadcasted_iota(jnp.int32, (1, cols * TILE), 1)
    lane_block = spread_lane % width // cols
    shares = 4
    size = n // shares
    line = lax.broadcasted_iota(jnp.int32, (NT * NB, size * cap), 0)

    def arrived(q, carry):
        record_copy(q).wait_recv()
        return carry

    for share in reversed(range(shares)):
        lax.fori_loop(share * size, min((share + 1) * size, n - 1), arrived, 0)
        x = rec[share * size : (share + 1) * size].reshape(size * cap, LANES)
        code_c = x[:, CODE_LANE : CODE_LANE + 1].astype(jnp.int32)
        code_r = x.T[CODE_LANE : CODE_LANE + 1, :].astype(jnp.int32)
        hi, lo = split2(x)
        tile_id = (
            lax.shift_right_logical(code_r, 10) % 8 * BAND + lax.shift_right_logical(code_r, 3) % 16
        )
        valid = code_r >= 8192
        src_r, dst_r = lax.shift_right_logical(code_r, 7) % 8, code_r % 8
        src_c, dst_c = lax.shift_right_logical(code_c, 7) % 8, code_c % 8
        for acc, spread, row_block, lane_of in (
            (acc_row, by_row, src_r, dst_c),
            (acc_col, by_col, dst_r, src_c),
        ):
            index = jnp.where(valid, tile_id * NB + row_block, -1)
            put = (line == index).astype(bf16)
            keep = lane_block == lane_of
            strips_hi = jnp.where(keep, mm(hi, spread), 0.0).astype(bf16)
            strips_lo = jnp.where(keep, mm(lo, spread), 0.0).astype(bf16)
            total = mm(put, strips_hi) + mm(put, strips_lo)
            if share == shares - 1:
                acc[...] = total
            else:
                acc[...] += total
    for dest, acc in ((rh, acc_row), (dh, acc_col)):
        for u in range(cols):
            dest[:, pl.ds(u, NB, stride=cols), :] = acc[:, u * TILE : (u + 1) * TILE].reshape(
                NT, NB, TILE
            )

    def sent_off(q, carry):
        record_copy(q).wait_send()
        return carry

    lax.fori_loop(0, n - 1, sent_off, 0)


def own_tiles():
    return [(i, j) for i in range(TILE_DEV) for j in range(TILE_DEV) if abs(i - j) <= HALF]


def tile_at(i, j):
    return i * BAND + j - i + HALF


LOW = [(a, b) for a in range(HALF) for b in range(HALF)]
LOW_PART = [(j, i) for j in range(HALF) for i in range(j - HALF, 0)]
HIGH_PART = [
    (j, i) for j in range(TILE_DEV - HALF, TILE_DEV) for i in range(TILE_DEV, j + HALF + 1)
]
CORNER = len(LOW)
PART = len(LOW_PART)
PAIRS = TILE_DEV // 2


def halo_of(i):
    return [j for j in range(i - HALF, i + HALF + 1) if not 0 <= j < TILE_DEV]


E_CHUNKS = [
    [t for t in own_tiles() if t[0] <= t[1]],
    [(i, j) for i in range(TILE_DEV) for j in halo_of(i)],
]
W_CHUNKS = [
    [
        (i, j)
        for i in (2 * p, 2 * p + 1)
        for j in range(i - HALF, i + HALF + 1)
        if not (0 <= j < i)
    ]
    for p in range(PAIRS)
]
E_AT = {t: n for n, t in enumerate(sum(E_CHUNKS, []))}
W_AT = {t: n for n, t in enumerate(sum(W_CHUNKS, []))}
SENT = len(E_AT)
HALO_SLOT = {t: n for n, t in enumerate(E_CHUNKS[1])}


def band_kernel(
    rows, groups, scale, dh_in, rh_in, out,
    dh, rh, le, lw, fe, fw, sp, rp, se, re, sw, rw, bhi, blo, ahi, alo, t1, sems, s_sem, r_sem,
):
    r = lax.axis_index("rows")
    g = lax.axis_index("feat")
    width = TILE // groups
    up, down = lax.rem(r + 1, rows), lax.rem(r + rows - 1, rows)
    y, c = g // 2, g % 2
    core_peer, y_peer = y * 2 + (1 - c), (1 - y) * 2 + c
    mine = pl.ds(pl.multiple_of(g * width, width), width)
    theirs = pl.ds(pl.multiple_of(y_peer * width, width), width)

    barrier = pltpu.get_barrier_semaphore()
    for who in ((up, g), (down, g), (r, core_peer), (r, y_peer)):
        pl.semaphore_signal(barrier, inc=1, device_id=who, device_id_type=MESH)

    rh_fetch = pltpu.make_async_copy(rh_in, rh, sems.at[0])
    dh_fetch = pltpu.make_async_copy(dh_in, dh, sems.at[1])
    rh_fetch.start()
    dh_fetch.start()

    def copy(src, dst, sem, who):
        return pltpu.make_async_remote_copy(
            src_ref=src, dst_ref=dst, send_sem=s_sem.at[sem], recv_sem=r_sem.at[sem],
            device_id=who, device_id_type=MESH,
        )

    pending = []

    def start(*args):
        item = copy(*args)
        item.start()
        pending.append(item)
        return item

    def gather(buf, first, size, sem):
        part = buf.at[pl.ds(first, size), mine]
        near = start(part, part, sem, (r, core_peer))
        far = start(part, part, sem + 1, (r, y_peer))
        return near, far, buf.at[pl.ds(first, size), theirs], sem + 2

    def forward(item):
        item[1].wait_recv()
        return start(item[2], item[2], item[3], (r, core_peer))

    def put_a(jj, kk, val):
        h, l = split2(val)
        ahi[jj * width : (jj + 1) * width, kk * TILE : (kk + 1) * TILE] = h
        alo[jj * width : (jj + 1) * width, kk * TILE : (kk + 1) * TILE] = l

    def put_b(kk, i, val):
        h, l = split2(val)
        bhi[kk * TILE : (kk + 1) * TILE, i * TILE : (i + 1) * TILE] = h
        blo[kk * TILE : (kk + 1) * TILE, i * TILE : (i + 1) * TILE] = l

    def build_own(buf, rows_of):
        for i in rows_of:
            for s in range(BAND):
                put_a(i + s, i + HALF, buf[i * BAND + s])

    def build_corner(recv, side):
        at = 0 if side == 0 else WIN - HALF
        for n, (a, b) in enumerate(LOW):
            put_a(b + at, a + at, recv[side, n])

    def build_tiles(buf, index, tiles):
        for i, j in tiles:
            full = buf[index[i, j]]
            put_b(j + HALF, i, full)
            if i != j:
                turned = full.T
                if 0 <= j < TILE_DEV:
                    put_b(i + HALF, j, turned)
                else:
                    t1[HALO_SLOT[i, j]] = turned
        for i, j in tiles:
            if not 0 <= j < TILE_DEV:
                put_a(i + HALF, j + HALF, t1[HALO_SLOT[i, j], mine, :])

    def product(p, emit):
        rows_at = slice(2 * p * width, (2 * p + 10) * width)
        mid = slice(2 * p * TILE, (2 * p + 10) * TILE)
        cols_at = slice(2 * p * TILE, (2 * p + 2) * TILE)
        a_h, b_h = ahi[rows_at, mid], bhi[mid, cols_at]
        acc = mm(a_h, b_h) + mm(a_h, blo[mid, cols_at]) + mm(alo[rows_at, mid], b_h)
        for di in range(2):
            for s in range(BAND):
                m = s + di
                emit(2 * p + di, s, acc[m * width : (m + 1) * width, di * TILE : (di + 1) * TILE])

    rh_fetch.wait()
    for n, (j, i) in enumerate(LOW_PART):
        sp[0, n] = rh[tile_at(j, i)]
    for n, (j, i) in enumerate(HIGH_PART):
        sp[1, n] = rh[tile_at(j, i)]
    pl.semaphore_wait(barrier, 4)
    part_low = start(sp.at[0], rp.at[1], 0, (down, g))
    part_high = start(sp.at[1], rp.at[0], 1, (up, g))
    dh_fetch.wait()
    for i, j in own_tiles():
        val = scale * (dh[tile_at(i, j)] + rh[tile_at(j, i)])
        le[tile_at(i, j)] = val
        if i <= j:
            fe[E_AT[i, j], mine, :] = val
    first_chunk = gather(fe, 0, len(E_CHUNKS[0]), 2)
    for n, (a, b) in enumerate(LOW):
        se[0, n] = le[tile_at(a, b)]
        se[1, n] = le[tile_at(a + HALF, b + HALF)]
    part_low.wait_recv()
    part_high.wait_recv()
    for n, (j, i) in enumerate(HIGH_PART):
        own, halo = i - TILE_DEV, j - TILE_DEV
        val = scale * (dh[tile_at(own, halo)] + rp[0, n])
        le[tile_at(own, halo)] = val
        fe[E_AT[own, halo], mine, :] = val
    for n, (j, i) in enumerate(LOW_PART):
        own, halo = i + TILE_DEV, j + TILE_DEV
        val = scale * (dh[tile_at(own, halo)] + rp[1, n])
        le[tile_at(own, halo)] = val
        fe[E_AT[own, halo], mine, :] = val
    second_chunk = gather(fe, len(E_CHUNKS[0]), len(E_CHUNKS[1]), 5)
    to_low = start(se.at[0], re.at[1], 8, (down, g))
    to_high = start(se.at[1], re.at[0], 9, (up, g))

    zero_block = jnp.zeros((TILE, TILE), bf16)
    for p in range(PAIRS):
        for i, kk in ((2 * p, 2 * p + 9), (2 * p + 1, 2 * p)):
            for ref in (bhi, blo):
                ref[kk * TILE : (kk + 1) * TILE, i * TILE : (i + 1) * TILE] = zero_block
    ahi[...] = jnp.zeros(ahi.shape, bf16)
    alo[...] = jnp.zeros(alo.shape, bf16)
    build_own(le, range(TILE_DEV))
    on = forward(first_chunk)
    first_chunk[0].wait_recv()
    on.wait_recv()
    build_tiles(fe, E_AT, E_CHUNKS[0])
    on = forward(second_chunk)
    second_chunk[0].wait_recv()
    on.wait_recv()
    build_tiles(fe, E_AT, E_CHUNKS[1])
    to_low.wait_recv()
    to_high.wait_recv()
    for side in range(2):
        build_corner(re, side)

    def first(i, s, acc):
        val = le[i * BAND + s] + acc
        lw[i * BAND + s] = val
        if (i, i + s - HALF) in W_AT:
            fw[W_AT[i, i + s - HALF], mine, :] = val

    chunks = []
    begin = 0
    corners = [None, None]
    for p in range(PAIRS):
        product(p, first)
        chunks.append(gather(fw, begin, len(W_CHUNKS[p]), 10 + 3 * p))
        begin += len(W_CHUNKS[p])
        if p == PAIRS // 2 - 1:
            for n, (a, b) in enumerate(LOW):
                sw[0, n] = lw[tile_at(a, b)]
            corners[1] = start(sw.at[0], rw.at[1], 22, (down, g))
    for n, (a, b) in enumerate(LOW):
        sw[1, n] = lw[tile_at(a + HALF, b + HALF)]
    corners[0] = start(sw.at[1], rw.at[0], 23, (up, g))
    build_own(lw, range(TILE_DEV))
    eye = (
        lax.broadcasted_iota(jnp.int32, (width, TILE), 0) + g * width
        == lax.broadcasted_iota(jnp.int32, (width, TILE), 1)
    ).astype(f32)

    def second(i, s, acc):
        val = 1.5 * lw[i * BAND + s] - acc
        if s == HALF:
            val = val + 0.4375 * eye
        out[i, s] = val

    for half in range(2):
        for p in (2 * half, 2 * half + 1):
            on = forward(chunks[p])
            chunks[p][0].wait_recv()
            on.wait_recv()
            build_tiles(fw, W_AT, W_CHUNKS[p])
        corners[half].wait_recv()
        build_corner(rw, half)
        for p in (2 * half, 2 * half + 1):
            product(p, second)
    for item in pending:
        item.wait_send()


def local(edge_feats, edge_owner, src_local, band_slot, dst_local, w_first, w_second, w_third):
    groups = lax.axis_size("feat")
    rows = lax.axis_size("rows")
    edges = edge_feats.shape[0]
    cap = max(2, 2 * edges // rows)
    width = TILE // groups
    tiles = (NT, width, TILE)
    vm = pl.BlockSpec(memory_space=pltpu.VMEM)
    anywhere = pl.BlockSpec(memory_space=pl.ANY)
    operands = (
        edge_feats, edge_owner.reshape(1, edges), src_local.reshape(1, edges),
        band_slot.reshape(1, edges), dst_local.reshape(1, edges), w_first, w_second, w_third,
    )
    partners = rows * groups
    sums = pltpu.VMEM((NT * NB, BLOCK // groups * TILE), f32)
    by_col, by_row = pl.pallas_call(
        functools.partial(route_kernel, rows, cap, groups),
        out_shape=[jax.ShapeDtypeStruct(tiles, f32)] * 2,
        in_specs=[anywhere] * len(operands),
        out_specs=[vm] * 2,
        scratch_shapes=[pltpu.VMEM(item.shape, item.dtype) for item in operands]
        + [
            pltpu.VMEM((rows, groups, cap, LANES), f32),
            pltpu.VMEM((partners, cap, LANES), f32),
            sums,
            sums,
            pltpu.SemaphoreType.DMA((len(operands),)),
            pltpu.SemaphoreType.DMA((partners,)),
            pltpu.SemaphoreType.DMA((partners,)),
        ],
        compiler_params=pltpu.CompilerParams(
            collective_id=0, has_side_effects=True, vmem_limit_bytes=56 << 20
        ),
    )(*operands)
    degree = groups * edges / (TILE_DEV * NB)
    scale = 0.5 * (0.5 / math.sqrt(2.0 * BLOCK * degree))
    return pl.pallas_call(
        functools.partial(band_kernel, rows, groups, scale),
        out_shape=jax.ShapeDtypeStruct((TILE_DEV, BAND, width, TILE), f32),
        in_specs=[anywhere] * 2,
        out_specs=vm,
        scratch_shapes=[pltpu.VMEM(tiles, f32)] * 4
        + [pltpu.VMEM((SENT, TILE, TILE), f32)] * 2
        + [pltpu.VMEM((2, PART, width, TILE), f32)] * 2
        + [pltpu.VMEM((2, CORNER, width, TILE), f32)] * 4
        + [pltpu.VMEM((WIN * TILE, TILE_DEV * TILE), bf16)] * 2
        + [pltpu.VMEM((WIN * width, WIN * TILE), bf16)] * 2
        + [pltpu.VMEM((len(HALO_SLOT), TILE, TILE), f32)]
        + [pltpu.SemaphoreType.DMA((2,))]
        + [pltpu.SemaphoreType.DMA((24,))] * 2,
        compiler_params=pltpu.CompilerParams(
            collective_id=1, has_side_effects=True, vmem_limit_bytes=60 << 20
        ),
    )(by_col, by_row)


def solution(mesh):
    in_specs = (
        P(("rows", "feat"), None),
        P(("rows", "feat"), None),
        P(("rows", "feat")),
        P(("rows", "feat")),
        P(("rows", "feat")),
        P(),
        P(),
        P(),
    )
    out_specs = P("rows", None, "feat", None)
    return jax.shard_map(local, mesh=mesh, in_specs=in_specs, out_specs=out_specs, check_vma=False)
```

```python
import functools
import math

import jax
import jax.numpy as jnp
from jax import lax
from jax.experimental import pallas as pl
from jax.experimental.pallas import tpu as pltpu
from jax.sharding import PartitionSpec as P

BLOCK = 16
TILE = 128
BAND = 9
TILE_DEV = 8
HALF = BAND // 2
NB = TILE // BLOCK
WIN = TILE_DEV + 2 * HALF
NT = TILE_DEV * BAND
LANES = 128
CODE_LANE = 112
MESH = pl.DeviceIdType.MESH
f32 = jnp.float32
bf16 = jnp.bfloat16


def split2(x):
    hi = x.astype(bf16)
    return hi, (x - hi.astype(f32)).astype(bf16)


def mm(a, b):
    return jnp.dot(a, b, preferred_element_type=f32)


def piece_columns(groups, cols):
    per = BLOCK * cols
    sub = cols * cols
    shape = (BLOCK * BLOCK, groups * LANES)
    source = lax.broadcasted_iota(jnp.int32, shape, 0)
    lane = lax.broadcasted_iota(jnp.int32, shape, 1)
    g, k = lane // LANES, lane % LANES
    other = (k - per) // sub
    other = other + (other >= g).astype(jnp.int32)
    from_row = other * per + g * sub + (k - per) % sub
    want = jnp.where(k < per, g * per + k, jnp.where(k < CODE_LANE, from_row, -1))
    return (source == want).astype(bf16)


def spread_columns(groups, cols, g):
    per = BLOCK * cols
    sub = cols * cols
    width = TILE // groups
    shape = (LANES, cols * TILE)
    source = lax.broadcasted_iota(jnp.int32, shape, 0)
    full = lax.broadcasted_iota(jnp.int32, shape, 1)
    u, lane = full // TILE, full % TILE
    other, unit = lane // width, lane % cols
    by_col = source == (other * cols + unit) * cols + u
    apart = per + (other - (other > g).astype(jnp.int32)) * sub + u * cols + unit
    by_row = source == jnp.where(other == g, (g * cols + u) * cols + unit, apart)
    return by_col.astype(bf16), by_row.astype(bf16)


def route_kernel(
    rows, cap, groups,
    feats_in, owner_in, src_in, slot_in, dst_in, w1_in, w2_in, w3_in, dh, rh,
    feats, owner_row, src_row, slot_row, dst_row, w1, w2, w3, sent, rec, acc_col, acc_row,
    sems, s_sem, r_sem,
):
    r = lax.axis_index("rows")
    g = lax.axis_index("feat")
    n = rows * groups
    edges = feats.shape[0]
    cols = BLOCK // groups
    width = TILE // groups

    def partner(q):
        turn = q // groups
        step = rows // 2 + (turn + 1) // 2 * (1 - 2 * (turn % 2))
        return (r + step + rows) % rows, (g + groups - 1 - q % groups) % groups

    def record_copy(q):
        to_row, to_group = partner(q)
        return pltpu.make_async_remote_copy(
            src_ref=sent.at[to_row, to_group], dst_ref=rec.at[q],
            send_sem=s_sem.at[q], recv_sem=r_sem.at[q],
            device_id=(to_row, to_group), device_id_type=MESH,
        )

    barrier = pltpu.get_barrier_semaphore()

    def greet(q, carry):
        pl.semaphore_signal(barrier, inc=1, device_id=partner(q), device_id_type=MESH)
        return carry

    lax.fori_loop(0, n - 1, greet, 0)

    fetches = []
    for k, (src, dst) in enumerate(
        (
            (feats_in, feats), (w1_in, w1), (w2_in, w2), (w3_in, w3), (owner_in, owner_row),
            (src_in, src_row), (slot_in, slot_row), (dst_in, dst_row),
        )
    ):
        fetch = pltpu.make_async_copy(src, dst, sems.at[k])
        fetch.start()
        fetches.append(fetch)
    perm = piece_columns(groups, cols)
    before = (
        lax.broadcasted_iota(jnp.int32, (edges, edges), 0)
        < lax.broadcasted_iota(jnp.int32, (edges, edges), 1)
    ).astype(bf16)
    for fetch in fetches:
        fetch.wait()
    h1 = mm(feats[...], w1[...])
    h1 = (h1 / (1.0 + jnp.exp(-h1))).astype(bf16)
    h2 = mm(h1, w2[...])
    h2 = (h2 / (1.0 + jnp.exp(-h2))).astype(bf16)
    w3p = mm(w3[...], perm).astype(bf16)
    vals = mm(h2, w3p)
    code = (8192 + src_row[...] * 128 + slot_row[...] * 8 + dst_row[...]).astype(f32)
    code_col = jnp.broadcast_to(code, (LANES, edges)).T[:, :1]
    lane = lax.broadcasted_iota(jnp.int32, vals.shape, 1)
    vals = jnp.where(lane % LANES == CODE_LANE, code_col, vals)
    owner = owner_row[...]
    names = (owner == lax.broadcasted_iota(jnp.int32, (rows, edges), 0)).astype(f32)
    rank = jnp.sum(names * mm(names.astype(bf16), before), axis=0, keepdims=True).astype(jnp.int32)
    target = owner * cap + rank
    place = (target == lax.broadcasted_iota(jnp.int32, (rows * cap, edges), 0)).astype(bf16)
    hi, lo = split2(vals)
    packed = mm(place, hi) + mm(place, lo)
    for k in range(groups):
        part = packed[:, k * LANES : (k + 1) * LANES]
        sent[:, k] = part.reshape(rows, cap, LANES)

    pl.semaphore_wait(barrier, n - 1)

    def send(q, carry):
        record_copy(q).start()
        return carry

    lax.fori_loop(0, n - 1, send, 0)
    rec[n - 1] = sent[r, g]

    by_col, by_row = spread_columns(groups, cols, g)
    spread_lane = lax.broadcasted_iota(jnp.int32, (1, cols * TILE), 1)
    lane_block = spread_lane % width // cols
    shares = 4
    size = n // shares
    line = lax.broadcasted_iota(jnp.int32, (NT * NB, size * cap), 0)

    def arrived(q, carry):
        record_copy(q).wait_recv()
        return carry

    for share in reversed(range(shares)):
        lax.fori_loop(share * size, min((share + 1) * size, n - 1), arrived, 0)
        x = rec[share * size : (share + 1) * size].reshape(size * cap, LANES)
        code_c = x[:, CODE_LANE : CODE_LANE + 1].astype(jnp.int32)
        code_r = x.T[CODE_LANE : CODE_LANE + 1, :].astype(jnp.int32)
        hi, lo = split2(x)
        tile_id = (
            lax.shift_right_logical(code_r, 10) % 8 * BAND + lax.shift_right_logical(code_r, 3) % 16
        )
        valid = code_r >= 8192
        src_r, dst_r = lax.shift_right_logical(code_r, 7) % 8, code_r % 8
        src_c, dst_c = lax.shift_right_logical(code_c, 7) % 8, code_c % 8
        for acc, spread, row_block, lane_of in (
            (acc_row, by_row, src_r, dst_c),
            (acc_col, by_col, dst_r, src_c),
        ):
            index = jnp.where(valid, tile_id * NB + row_block, -1)
            put = (line == index).astype(bf16)
            keep = lane_block == lane_of
            strips_hi = jnp.where(keep, mm(hi, spread), 0.0).astype(bf16)
            strips_lo = jnp.where(keep, mm(lo, spread), 0.0).astype(bf16)
            total = mm(put, strips_hi) + mm(put, strips_lo)
            if share == shares - 1:
                acc[...] = total
            else:
                acc[...] += total
    for dest, acc in ((rh, acc_row), (dh, acc_col)):
        for u in range(cols):
            dest[:, pl.ds(u, NB, stride=cols), :] = acc[:, u * TILE : (u + 1) * TILE].reshape(
                NT, NB, TILE
            )

    def sent_off(q, carry):
        record_copy(q).wait_send()
        return carry

    lax.fori_loop(0, n - 1, sent_off, 0)


def own_tiles():
    return [(i, j) for i in range(TILE_DEV) for j in range(TILE_DEV) if abs(i - j) <= HALF]


def tile_at(i, j):
    return i * BAND + j - i + HALF


LOW = [(a, b) for a in range(HALF) for b in range(HALF)]
LOW_PART = [(j, i) for j in range(HALF) for i in range(j - HALF, 0)]
HIGH_PART = [
    (j, i) for j in range(TILE_DEV - HALF, TILE_DEV) for i in range(TILE_DEV, j + HALF + 1)
]
CORNER = len(LOW)
PART = len(LOW_PART)
PAIRS = TILE_DEV // 2


def halo_of(i):
    return [j for j in range(i - HALF, i + HALF + 1) if not 0 <= j < TILE_DEV]


E_CHUNKS = [
    [t for t in own_tiles() if t[0] <= t[1]],
    [(i, j) for i in range(TILE_DEV) for j in halo_of(i)],
]
E_AT = {t: n for n, t in enumerate(sum(E_CHUNKS, []))}
SENT = len(E_AT)
OWN = len(E_CHUNKS[0])
SIDE = len(E_CHUNKS[1]) // 2
SIDES = [E_CHUNKS[1][:SIDE], E_CHUNKS[1][SIDE:]]
HALO_SLOT = {t: n for n, t in enumerate(E_CHUNKS[1])}
OWN_SLOT = {t: n for n, t in enumerate(t for t in E_CHUNKS[0] if t[0] != t[1])}


def band_kernel(
    rows, groups, scale, dh_in, rh_in, out,
    dh, rh, le, lw, fe, fw, sp, rp, se, re, sw, rw, bhi, blo, fhi, flo, ahi, alo, t1, tw, sems, s_sem, r_sem,
):
    r = lax.axis_index("rows")
    g = lax.axis_index("feat")
    width = TILE // groups
    up, down = lax.rem(r + 1, rows), lax.rem(r + rows - 1, rows)
    y, c = g // 2, g % 2
    core_peer, y_peer = y * 2 + (1 - c), (1 - y) * 2 + c
    mine = pl.ds(pl.multiple_of(g * width, width), width)
    theirs = pl.ds(pl.multiple_of(y_peer * width, width), width)

    barrier = pltpu.get_barrier_semaphore()
    for who in ((up, g), (down, g), (r, core_peer), (r, y_peer)):
        pl.semaphore_signal(barrier, inc=1, device_id=who, device_id_type=MESH)

    rh_fetch = pltpu.make_async_copy(rh_in, rh, sems.at[0])
    dh_fetch = pltpu.make_async_copy(dh_in, dh, sems.at[1])
    rh_fetch.start()
    dh_fetch.start()

    def copy(src, dst, sem, who):
        return pltpu.make_async_remote_copy(
            src_ref=src, dst_ref=dst, send_sem=s_sem.at[sem], recv_sem=r_sem.at[sem],
            device_id=who, device_id_type=MESH,
        )

    pending = []

    def start(*args):
        item = copy(*args)
        item.start()
        pending.append(item)
        return item

    def gather(buf, first, size, sem):
        part = buf.at[pl.ds(first, size), mine]
        near = start(part, part, sem, (r, core_peer))
        far = start(part, part, sem + 1, (r, y_peer))
        return near, far, buf.at[pl.ds(first, size), theirs], sem + 2

    def forward(item):
        item[1].wait_recv()
        return start(item[2], item[2], item[3], (r, core_peer))

    def put_a(jj, kk, val):
        h, l = split2(val)
        ahi[jj * width : (jj + 1) * width, kk * TILE : (kk + 1) * TILE] = h
        alo[jj * width : (jj + 1) * width, kk * TILE : (kk + 1) * TILE] = l

    def put(refs, row, col, parts):
        for ref, part in zip(refs, parts):
            ref[row * TILE : (row + 1) * TILE, col * TILE : (col + 1) * TILE] = part

    right, left = (bhi, blo), (fhi, flo)

    def build_corner(recv, side):
        at = 0 if side == 0 else WIN - HALF
        for n, (a, b) in enumerate(LOW):
            put_a(b + at, a + at, recv[side, n])

    def build_start(tiles):
        for i, j in tiles:
            full = fe[E_AT[i, j]]
            parts = split2(full)
            put(right, j + HALF, i, parts)
            inside = 0 <= j < TILE_DEV
            if inside:
                put(left, j, i + HALF, parts)
            if i != j:
                turned = split2(full.T)
                put(left, i, j + HALF, turned)
                if inside:
                    put(right, i + HALF, j, turned)

    def build_own_square():
        for i, j in E_CHUNKS[0]:
            put(right, j + HALF, i, split2(fw[E_AT[i, j]]))
            if i != j:
                put(right, i + HALF, j, split2(tw[OWN_SLOT[i, j]]))

    def build_side(tiles):
        for i, j in tiles:
            full = fw[E_AT[i, j]]
            put(right, j + HALF, i, split2(full))
            t1[HALO_SLOT[i, j]] = full.T
        for i, j in tiles:
            put_a(i + HALF, j + HALF, t1[HALO_SLOT[i, j], mine, :])

    def three(ref_l, at_l, ref_r, at_r):
        a_h, b_h = ref_l[0][at_l], ref_r[0][at_r]
        return mm(a_h, b_h) + mm(a_h, ref_r[1][at_r]) + mm(ref_l[1][at_l], b_h)

    def square(p, q):
        mid = slice(2 * q * TILE, (2 * p + 10) * TILE)
        acc = three(
            left, (slice(2 * q * TILE, (2 * q + 2) * TILE), mid),
            right, (mid, slice(2 * p * TILE, (2 * p + 2) * TILE)),
        )
        for di in range(2):
            for dj in range(2):
                i, j = 2 * p + di, 2 * q + dj
                if (i, j) in E_AT:
                    n = E_AT[i, j]
                    val = fe[n] + acc[dj * TILE : (dj + 1) * TILE, di * TILE : (di + 1) * TILE]
                    fw[n] = val
                    if i != j:
                        tw[OWN_SLOT[i, j]] = val.T

    def own_parts(tiles):
        for i, j in tiles:
            lw[tile_at(i, j)] = fw[E_AT[i, j], mine, :]
            if i != j:
                lw[tile_at(j, i)] = tw[OWN_SLOT[i, j], mine, :]

    def halo_side(side):
        jj0 = 0 if side == 0 else WIN - HALF
        mid = slice(0, TILE_DEV * TILE) if side == 0 else slice(TILE_DEV * TILE, WIN * TILE)
        i0 = 0 if side == 0 else TILE_DEV - HALF
        acc = three(
            (ahi, alo), (slice(jj0 * width, (jj0 + HALF) * width), mid),
            right, (mid, slice(i0 * TILE, (i0 + HALF) * TILE)),
        )
        for i, j in SIDES[side]:
            m = j + HALF - jj0
            val = le[tile_at(i, j)] + acc[
                m * width : (m + 1) * width, (i - i0) * TILE : (i - i0 + 1) * TILE
            ]
            lw[tile_at(i, j)] = val
            fw[E_AT[i, j], mine, :] = val

    def product(p, emit):
        rows_at = slice(2 * p * width, (2 * p + 10) * width)
        mid = slice(2 * p * TILE, (2 * p + 10) * TILE)
        cols_at = slice(2 * p * TILE, (2 * p + 2) * TILE)
        acc = three((ahi, alo), (rows_at, mid), right, (mid, cols_at))
        for di in range(2):
            for s in range(BAND):
                m = s + di
                emit(2 * p + di, s, acc[m * width : (m + 1) * width, di * TILE : (di + 1) * TILE])

    rh_fetch.wait()
    for n, (j, i) in enumerate(LOW_PART):
        sp[0, n] = rh[tile_at(j, i)]
    for n, (j, i) in enumerate(HIGH_PART):
        sp[1, n] = rh[tile_at(j, i)]
    pl.semaphore_wait(barrier, 4)
    part_low = start(sp.at[0], rp.at[1], 0, (down, g))
    part_high = start(sp.at[1], rp.at[0], 1, (up, g))
    dh_fetch.wait()
    for i, j in own_tiles():
        val = scale * (dh[tile_at(i, j)] + rh[tile_at(j, i)])
        le[tile_at(i, j)] = val
        if i <= j:
            fe[E_AT[i, j], mine, :] = val
    first_chunk = gather(fe, 0, len(E_CHUNKS[0]), 2)
    for n, (a, b) in enumerate(LOW):
        se[0, n] = le[tile_at(a, b)]
        se[1, n] = le[tile_at(a + HALF, b + HALF)]
    part_low.wait_recv()
    part_high.wait_recv()
    for n, (j, i) in enumerate(HIGH_PART):
        own, halo = i - TILE_DEV, j - TILE_DEV
        val = scale * (dh[tile_at(own, halo)] + rp[0, n])
        le[tile_at(own, halo)] = val
        fe[E_AT[own, halo], mine, :] = val
    for n, (j, i) in enumerate(LOW_PART):
        own, halo = i + TILE_DEV, j + TILE_DEV
        val = scale * (dh[tile_at(own, halo)] + rp[1, n])
        le[tile_at(own, halo)] = val
        fe[E_AT[own, halo], mine, :] = val
    second_chunk = gather(fe, len(E_CHUNKS[0]), len(E_CHUNKS[1]), 5)
    to_low = start(se.at[0], re.at[1], 8, (down, g))
    to_high = start(se.at[1], re.at[0], 9, (up, g))

    zero_block = jnp.zeros((TILE, TILE), bf16)
    empty = set()
    for p in range(PAIRS):
        empty |= {(2 * p + 9, 2 * p), (2 * p, 2 * p + 1)}
    for i in range(HALF):
        empty |= {(kk, i) for kk in range(i)}
        empty |= {(kk, i + HALF) for kk in range(i + HALF + BAND, WIN)}
    for kk, i in sorted(empty):
        put(right, kk, i, (zero_block, zero_block))
    for p in range(PAIRS):
        put(left, 2 * p, 2 * p + 9, (zero_block, zero_block))
        put(left, 2 * p + 1, 2 * p, (zero_block, zero_block))
    ahi[...] = jnp.zeros(ahi.shape, bf16)
    alo[...] = jnp.zeros(alo.shape, bf16)
    for i in range(TILE_DEV):
        for j in halo_of(i):
            put_a(j + HALF, i + HALF, le[tile_at(i, j)])
    on = forward(first_chunk)
    first_chunk[0].wait_recv()
    on.wait_recv()
    build_start(E_CHUNKS[0])
    for p, q in ((0, 2), (1, 2), (1, 3)):
        square(p, q)
    on = forward(second_chunk)
    second_chunk[0].wait_recv()
    on.wait_recv()
    build_start(E_CHUNKS[1])

    corners = [None, None]
    for p, q in ((0, 0), (0, 1), (1, 1)):
        square(p, q)
    own_parts([t for t in E_CHUNKS[0] if t[1] < HALF])
    for n, (a, b) in enumerate(LOW):
        sw[0, n] = lw[tile_at(a, b)]
    corners[1] = start(sw.at[0], rw.at[1], 13, (down, g))
    for p, q in ((2, 2), (2, 3), (3, 3)):
        square(p, q)
    own_parts([t for t in E_CHUNKS[0] if t[0] >= HALF])
    for n, (a, b) in enumerate(LOW):
        sw[1, n] = lw[tile_at(a + HALF, b + HALF)]
    corners[0] = start(sw.at[1], rw.at[0], 14, (up, g))
    own_parts([t for t in E_CHUNKS[0] if t[0] < HALF <= t[1]])

    chunks = []
    halos = (to_high, to_low)
    for side in range(2):
        halos[side].wait_recv()
        build_corner(re, side)
        halo_side(side)
        chunks.append(gather(fw, OWN + side * SIDE, SIDE, (10, 15)[side]))
    build_own_square()
    for i in range(TILE_DEV):
        for s in range(BAND):
            put_a(i + s, i + HALF, lw[i * BAND + s])
    eye = (
        lax.broadcasted_iota(jnp.int32, (width, TILE), 0) + g * width
        == lax.broadcasted_iota(jnp.int32, (width, TILE), 1)
    ).astype(f32)

    def second(i, s, acc):
        val = 1.5 * lw[i * BAND + s] - acc
        if s == HALF:
            val = val + 0.4375 * eye
        out[i, s] = val

    for half in range(2):
        on = forward(chunks[half])
        chunks[half][0].wait_recv()
        on.wait_recv()
        build_side(SIDES[half])
        corners[half].wait_recv()
        build_corner(rw, half)
        for p in (2 * half, 2 * half + 1):
            product(p, second)
    for item in pending:
        item.wait_send()


def local(edge_feats, edge_owner, src_local, band_slot, dst_local, w_first, w_second, w_third):
    groups = lax.axis_size("feat")
    rows = lax.axis_size("rows")
    edges = edge_feats.shape[0]
    cap = max(2, 2 * edges // rows)
    width = TILE // groups
    tiles = (NT, width, TILE)
    vm = pl.BlockSpec(memory_space=pltpu.VMEM)
    anywhere = pl.BlockSpec(memory_space=pl.ANY)
    operands = (
        edge_feats, edge_owner.reshape(1, edges), src_local.reshape(1, edges),
        band_slot.reshape(1, edges), dst_local.reshape(1, edges), w_first, w_second, w_third,
    )
    partners = rows * groups
    sums = pltpu.VMEM((NT * NB, BLOCK // groups * TILE), f32)
    by_col, by_row = pl.pallas_call(
        functools.partial(route_kernel, rows, cap, groups),
        out_shape=[jax.ShapeDtypeStruct(tiles, f32)] * 2,
        in_specs=[anywhere] * len(operands),
        out_specs=[vm] * 2,
        scratch_shapes=[pltpu.VMEM(item.shape, item.dtype) for item in operands]
        + [
            pltpu.VMEM((rows, groups, cap, LANES), f32),
            pltpu.VMEM((partners, cap, LANES), f32),
            sums,
            sums,
            pltpu.SemaphoreType.DMA((len(operands),)),
            pltpu.SemaphoreType.DMA((partners,)),
            pltpu.SemaphoreType.DMA((partners,)),
        ],
        compiler_params=pltpu.CompilerParams(
            collective_id=0, has_side_effects=True, vmem_limit_bytes=56 << 20
        ),
    )(*operands)
    degree = groups * edges / (TILE_DEV * NB)
    scale = 0.5 * (0.5 / math.sqrt(2.0 * BLOCK * degree))
    return pl.pallas_call(
        functools.partial(band_kernel, rows, groups, scale),
        out_shape=jax.ShapeDtypeStruct((TILE_DEV, BAND, width, TILE), f32),
        in_specs=[anywhere] * 2,
        out_specs=vm,
        scratch_shapes=[pltpu.VMEM(tiles, f32)] * 4
        + [pltpu.VMEM((SENT, TILE, TILE), f32)] * 2
        + [pltpu.VMEM((2, PART, width, TILE), f32)] * 2
        + [pltpu.VMEM((2, CORNER, width, TILE), f32)] * 4
        + [pltpu.VMEM((WIN * TILE, TILE_DEV * TILE), bf16)] * 2
        + [pltpu.VMEM((TILE_DEV * TILE, WIN * TILE), bf16)] * 2
        + [pltpu.VMEM((WIN * width, WIN * TILE), bf16)] * 2
        + [pltpu.VMEM((len(HALO_SLOT), TILE, TILE), f32)]
        + [pltpu.VMEM((len(OWN_SLOT), TILE, TILE), f32)]
        + [pltpu.SemaphoreType.DMA((2,))]
        + [pltpu.SemaphoreType.DMA((18,))] * 2,
        compiler_params=pltpu.CompilerParams(
            collective_id=1, has_side_effects=True, vmem_limit_bytes=60 << 20
        ),
    )(by_col, by_row)


def solution(mesh):
    in_specs = (
        P(("rows", "feat"), None),
        P(("rows", "feat"), None),
        P(("rows", "feat")),
        P(("rows", "feat")),
        P(("rows", "feat")),
        P(),
        P(),
        P(),
    )
    out_specs = P("rows", None, "feat", None)
    return jax.shard_map(local, mesh=mesh, in_specs=in_specs, out_specs=out_specs, check_vma=False)
```

```python
import functools
import math

import jax
import jax.numpy as jnp
from jax import lax
from jax.experimental import pallas as pl
from jax.experimental.pallas import tpu as pltpu
from jax.sharding import PartitionSpec as P

BLOCK = 16
TILE = 128
BAND = 9
TILE_DEV = 8
HALF = BAND // 2
NB = TILE // BLOCK
WIN = TILE_DEV + 2 * HALF
NT = TILE_DEV * BAND
LANES = 128
CODE_LANE = 112
MESH = pl.DeviceIdType.MESH
f32 = jnp.float32
bf16 = jnp.bfloat16


def split2(x):
    hi = x.astype(bf16)
    return hi, (x - hi.astype(f32)).astype(bf16)


def mm(a, b):
    return jnp.dot(a, b, preferred_element_type=f32)


def piece_columns(groups, cols):
    per = BLOCK * cols
    sub = cols * cols
    shape = (BLOCK * BLOCK, groups * LANES)
    source = lax.broadcasted_iota(jnp.int32, shape, 0)
    lane = lax.broadcasted_iota(jnp.int32, shape, 1)
    g, k = lane // LANES, lane % LANES
    other = (k - per) // sub
    other = other + (other >= g).astype(jnp.int32)
    from_row = other * per + g * sub + (k - per) % sub
    want = jnp.where(k < per, g * per + k, jnp.where(k < CODE_LANE, from_row, -1))
    return (source == want).astype(bf16)


def spread_columns(groups, cols, g):
    per = BLOCK * cols
    sub = cols * cols
    width = TILE // groups
    shape = (LANES, cols * TILE)
    source = lax.broadcasted_iota(jnp.int32, shape, 0)
    full = lax.broadcasted_iota(jnp.int32, shape, 1)
    u, lane = full // TILE, full % TILE
    other, unit = lane // width, lane % cols
    by_col = source == (other * cols + unit) * cols + u
    apart = per + (other - (other > g).astype(jnp.int32)) * sub + u * cols + unit
    by_row = source == jnp.where(other == g, (g * cols + u) * cols + unit, apart)
    return by_col.astype(bf16), by_row.astype(bf16)


def route_kernel(
    rows, cap, groups,
    feats_in, owner_in, src_in, slot_in, dst_in, w1_in, w2_in, w3_in, dh, rh,
    feats, owner_row, src_row, slot_row, dst_row, w1, w2, w3, sent, rec, acc_col, acc_row,
    sems, s_sem, r_sem,
):
    r = lax.axis_index("rows")
    g = lax.axis_index("feat")
    n = rows * groups
    edges = feats.shape[0]
    cols = BLOCK // groups
    width = TILE // groups

    def partner(q):
        turn = q // groups
        step = rows // 2 + (turn + 1) // 2 * (1 - 2 * (turn % 2))
        return (r + step + rows) % rows, (g + groups - 1 - q % groups) % groups

    def record_copy(q):
        to_row, to_group = partner(q)
        return pltpu.make_async_remote_copy(
            src_ref=sent.at[to_row, to_group], dst_ref=rec.at[q],
            send_sem=s_sem.at[q], recv_sem=r_sem.at[q],
            device_id=(to_row, to_group), device_id_type=MESH,
        )

    barrier = pltpu.get_barrier_semaphore()

    def greet(q, carry):
        pl.semaphore_signal(barrier, inc=1, device_id=partner(q), device_id_type=MESH)
        return carry

    lax.fori_loop(0, n - 1, greet, 0)

    fetches = []
    for k, (src, dst) in enumerate(
        (
            (feats_in, feats), (w1_in, w1), (w2_in, w2), (w3_in, w3), (owner_in, owner_row),
            (src_in, src_row), (slot_in, slot_row), (dst_in, dst_row),
        )
    ):
        fetch = pltpu.make_async_copy(src, dst, sems.at[k])
        fetch.start()
        fetches.append(fetch)
    perm = piece_columns(groups, cols)
    before = (
        lax.broadcasted_iota(jnp.int32, (edges, edges), 0)
        < lax.broadcasted_iota(jnp.int32, (edges, edges), 1)
    ).astype(bf16)
    for fetch in fetches:
        fetch.wait()
    h1 = mm(feats[...], w1[...])
    h1 = (h1 / (1.0 + jnp.exp(-h1))).astype(bf16)
    h2 = mm(h1, w2[...])
    h2 = (h2 / (1.0 + jnp.exp(-h2))).astype(bf16)
    w3p = mm(w3[...], perm).astype(bf16)
    vals = mm(h2, w3p)
    code = (8192 + src_row[...] * 128 + slot_row[...] * 8 + dst_row[...]).astype(f32)
    code_col = jnp.broadcast_to(code, (LANES, edges)).T[:, :1]
    lane = lax.broadcasted_iota(jnp.int32, vals.shape, 1)
    vals = jnp.where(lane % LANES == CODE_LANE, code_col, vals)
    owner = owner_row[...]
    names = (owner == lax.broadcasted_iota(jnp.int32, (rows, edges), 0)).astype(f32)
    rank = jnp.sum(names * mm(names.astype(bf16), before), axis=0, keepdims=True).astype(jnp.int32)
    target = owner * cap + rank
    place = (target == lax.broadcasted_iota(jnp.int32, (rows * cap, edges), 0)).astype(bf16)
    hi, lo = split2(vals)
    packed = mm(place, hi) + mm(place, lo)
    for k in range(groups):
        part = packed[:, k * LANES : (k + 1) * LANES]
        sent[:, k] = part.reshape(rows, cap, LANES)

    pl.semaphore_wait(barrier, n - 1)

    def send(q, carry):
        record_copy(q).start()
        return carry

    lax.fori_loop(0, n - 1, send, 0)
    rec[n - 1] = sent[r, g]

    by_col, by_row = spread_columns(groups, cols, g)
    spread_lane = lax.broadcasted_iota(jnp.int32, (1, cols * TILE), 1)
    lane_block = spread_lane % width // cols
    shares = 4
    size = n // shares
    line = lax.broadcasted_iota(jnp.int32, (NT * NB, size * cap), 0)

    def arrived(q, carry):
        record_copy(q).wait_recv()
        return carry

    for share in reversed(range(shares)):
        lax.fori_loop(share * size, min((share + 1) * size, n - 1), arrived, 0)
        x = rec[share * size : (share + 1) * size].reshape(size * cap, LANES)
        code_c = x[:, CODE_LANE : CODE_LANE + 1].astype(jnp.int32)
        code_r = x.T[CODE_LANE : CODE_LANE + 1, :].astype(jnp.int32)
        hi, lo = split2(x)
        tile_id = (
            lax.shift_right_logical(code_r, 10) % 8 * BAND + lax.shift_right_logical(code_r, 3) % 16
        )
        valid = code_r >= 8192
        src_r, dst_r = lax.shift_right_logical(code_r, 7) % 8, code_r % 8
        src_c, dst_c = lax.shift_right_logical(code_c, 7) % 8, code_c % 8
        for acc, spread, row_block, lane_of in (
            (acc_row, by_row, src_r, dst_c),
            (acc_col, by_col, dst_r, src_c),
        ):
            index = jnp.where(valid, tile_id * NB + row_block, -1)
            put = (line == index).astype(bf16)
            keep = lane_block == lane_of
            strips_hi = jnp.where(keep, mm(hi, spread), 0.0).astype(bf16)
            strips_lo = jnp.where(keep, mm(lo, spread), 0.0).astype(bf16)
            total = mm(put, strips_hi) + mm(put, strips_lo)
            if share == shares - 1:
                acc[...] = total
            else:
                acc[...] += total
    for dest, acc in ((rh, acc_row), (dh, acc_col)):
        for u in range(cols):
            dest[:, pl.ds(u, NB, stride=cols), :] = acc[:, u * TILE : (u + 1) * TILE].reshape(
                NT, NB, TILE
            )

    def sent_off(q, carry):
        record_copy(q).wait_send()
        return carry

    lax.fori_loop(0, n - 1, sent_off, 0)


def own_tiles():
    return [(i, j) for i in range(TILE_DEV) for j in range(TILE_DEV) if abs(i - j) <= HALF]


def tile_at(i, j):
    return i * BAND + j - i + HALF


LOW = [(a, b) for a in range(HALF) for b in range(HALF)]
LOW_PART = [(j, i) for j in range(HALF) for i in range(j - HALF, 0)]
HIGH_PART = [
    (j, i) for j in range(TILE_DEV - HALF, TILE_DEV) for i in range(TILE_DEV, j + HALF + 1)
]
CORNER = len(LOW)
PART = len(LOW_PART)
PAIRS = TILE_DEV // 2


def halo_of(i):
    return [j for j in range(i - HALF, i + HALF + 1) if not 0 <= j < TILE_DEV]


E_CHUNKS = [
    [t for t in own_tiles() if t[0] <= t[1]],
    [(i, j) for i in range(TILE_DEV) for j in halo_of(i)],
]
E_AT = {t: n for n, t in enumerate(sum(E_CHUNKS, []))}
SENT = len(E_AT)
OWN = len(E_CHUNKS[0])
SIDE = len(E_CHUNKS[1]) // 2
SIDES = [E_CHUNKS[1][:SIDE], E_CHUNKS[1][SIDE:]]
HALO_SLOT = {t: n for n, t in enumerate(E_CHUNKS[1])}
OWN_SLOT = {t: n for n, t in enumerate(t for t in E_CHUNKS[0] if t[0] != t[1])}


def band_kernel(
    rows, groups, scale, out,
    dh, rh, le, lw, fe, fw, sp, rp, se, re, sw, rw, bhi, blo, fhi, flo, ahi, alo, t1, tw, s_sem, r_sem,
):
    r = lax.axis_index("rows")
    g = lax.axis_index("feat")
    width = TILE // groups
    up, down = lax.rem(r + 1, rows), lax.rem(r + rows - 1, rows)
    y, c = g // 2, g % 2
    core_peer, y_peer = y * 2 + (1 - c), (1 - y) * 2 + c
    mine = pl.ds(pl.multiple_of(g * width, width), width)
    theirs = pl.ds(pl.multiple_of(y_peer * width, width), width)

    def copy(src, dst, sem, who):
        return pltpu.make_async_remote_copy(
            src_ref=src, dst_ref=dst, send_sem=s_sem.at[sem], recv_sem=r_sem.at[sem],
            device_id=who, device_id_type=MESH,
        )

    pending = []

    def start(*args):
        item = copy(*args)
        item.start()
        pending.append(item)
        return item

    def gather(buf, first, size, sem):
        part = buf.at[pl.ds(first, size), mine]
        near = start(part, part, sem, (r, core_peer))
        far = start(part, part, sem + 1, (r, y_peer))
        return near, far, buf.at[pl.ds(first, size), theirs], sem + 2

    def forward(item):
        item[1].wait_recv()
        return start(item[2], item[2], item[3], (r, core_peer))

    def put_a(jj, kk, val):
        h, l = split2(val)
        ahi[jj * width : (jj + 1) * width, kk * TILE : (kk + 1) * TILE] = h
        alo[jj * width : (jj + 1) * width, kk * TILE : (kk + 1) * TILE] = l

    def put(refs, row, col, parts):
        for ref, part in zip(refs, parts):
            ref[row * TILE : (row + 1) * TILE, col * TILE : (col + 1) * TILE] = part

    right, left = (bhi, blo), (fhi, flo)

    def build_corner(recv, side):
        at = 0 if side == 0 else WIN - HALF
        for n, (a, b) in enumerate(LOW):
            put_a(b + at, a + at, recv[side, n])

    def build_start(tiles):
        for i, j in tiles:
            full = fe[E_AT[i, j]]
            parts = split2(full)
            put(right, j + HALF, i, parts)
            inside = 0 <= j < TILE_DEV
            if inside:
                put(left, j, i + HALF, parts)
            if i != j:
                turned = split2(full.T)
                put(left, i, j + HALF, turned)
                if inside:
                    put(right, i + HALF, j, turned)

    def build_own_square():
        for i, j in E_CHUNKS[0]:
            put(right, j + HALF, i, split2(fw[E_AT[i, j]]))
            if i != j:
                put(right, i + HALF, j, split2(tw[OWN_SLOT[i, j]]))

    def build_side(tiles):
        for i, j in tiles:
            full = fw[E_AT[i, j]]
            put(right, j + HALF, i, split2(full))
            t1[HALO_SLOT[i, j]] = full.T
        for i, j in tiles:
            put_a(i + HALF, j + HALF, t1[HALO_SLOT[i, j], mine, :])

    def three(ref_l, at_l, ref_r, at_r):
        a_h, b_h = ref_l[0][at_l], ref_r[0][at_r]
        return mm(a_h, b_h) + mm(a_h, ref_r[1][at_r]) + mm(ref_l[1][at_l], b_h)

    def square(p, q):
        mid = slice(2 * q * TILE, (2 * p + 10) * TILE)
        acc = three(
            left, (slice(2 * q * TILE, (2 * q + 2) * TILE), mid),
            right, (mid, slice(2 * p * TILE, (2 * p + 2) * TILE)),
        )
        for di in range(2):
            for dj in range(2):
                i, j = 2 * p + di, 2 * q + dj
                if (i, j) in E_AT:
                    n = E_AT[i, j]
                    val = fe[n] + acc[dj * TILE : (dj + 1) * TILE, di * TILE : (di + 1) * TILE]
                    fw[n] = val
                    if i != j:
                        tw[OWN_SLOT[i, j]] = val.T

    def own_parts(tiles):
        for i, j in tiles:
            lw[tile_at(i, j)] = fw[E_AT[i, j], mine, :]
            if i != j:
                lw[tile_at(j, i)] = tw[OWN_SLOT[i, j], mine, :]

    def halo_side(side):
        jj0 = 0 if side == 0 else WIN - HALF
        mid = slice(0, TILE_DEV * TILE) if side == 0 else slice(TILE_DEV * TILE, WIN * TILE)
        i0 = 0 if side == 0 else TILE_DEV - HALF
        acc = three(
            (ahi, alo), (slice(jj0 * width, (jj0 + HALF) * width), mid),
            right, (mid, slice(i0 * TILE, (i0 + HALF) * TILE)),
        )
        for i, j in SIDES[side]:
            m = j + HALF - jj0
            val = le[tile_at(i, j)] + acc[
                m * width : (m + 1) * width, (i - i0) * TILE : (i - i0 + 1) * TILE
            ]
            lw[tile_at(i, j)] = val
            fw[E_AT[i, j], mine, :] = val

    def product(p, emit):
        rows_at = slice(2 * p * width, (2 * p + 10) * width)
        mid = slice(2 * p * TILE, (2 * p + 10) * TILE)
        cols_at = slice(2 * p * TILE, (2 * p + 2) * TILE)
        acc = three((ahi, alo), (rows_at, mid), right, (mid, cols_at))
        for di in range(2):
            for s in range(BAND):
                m = s + di
                emit(2 * p + di, s, acc[m * width : (m + 1) * width, di * TILE : (di + 1) * TILE])

    for n, (j, i) in enumerate(LOW_PART):
        sp[0, n] = rh[tile_at(j, i)]
    for n, (j, i) in enumerate(HIGH_PART):
        sp[1, n] = rh[tile_at(j, i)]
    part_low = start(sp.at[0], rp.at[1], 0, (down, g))
    part_high = start(sp.at[1], rp.at[0], 1, (up, g))
    for i, j in own_tiles():
        val = scale * (dh[tile_at(i, j)] + rh[tile_at(j, i)])
        le[tile_at(i, j)] = val
        if i <= j:
            fe[E_AT[i, j], mine, :] = val
    first_chunk = gather(fe, 0, len(E_CHUNKS[0]), 2)
    for n, (a, b) in enumerate(LOW):
        se[0, n] = le[tile_at(a, b)]
        se[1, n] = le[tile_at(a + HALF, b + HALF)]
    part_low.wait_recv()
    part_high.wait_recv()
    for n, (j, i) in enumerate(HIGH_PART):
        own, halo = i - TILE_DEV, j - TILE_DEV
        val = scale * (dh[tile_at(own, halo)] + rp[0, n])
        le[tile_at(own, halo)] = val
        fe[E_AT[own, halo], mine, :] = val
    for n, (j, i) in enumerate(LOW_PART):
        own, halo = i + TILE_DEV, j + TILE_DEV
        val = scale * (dh[tile_at(own, halo)] + rp[1, n])
        le[tile_at(own, halo)] = val
        fe[E_AT[own, halo], mine, :] = val
    second_chunk = gather(fe, len(E_CHUNKS[0]), len(E_CHUNKS[1]), 5)
    to_low = start(se.at[0], re.at[1], 8, (down, g))
    to_high = start(se.at[1], re.at[0], 9, (up, g))

    zero_block = jnp.zeros((TILE, TILE), bf16)
    empty = set()
    for p in range(PAIRS):
        empty |= {(2 * p + 9, 2 * p), (2 * p, 2 * p + 1)}
    for i in range(HALF):
        empty |= {(kk, i) for kk in range(i)}
        empty |= {(kk, i + HALF) for kk in range(i + HALF + BAND, WIN)}
    for kk, i in sorted(empty):
        put(right, kk, i, (zero_block, zero_block))
    for p in range(PAIRS):
        put(left, 2 * p, 2 * p + 9, (zero_block, zero_block))
        put(left, 2 * p + 1, 2 * p, (zero_block, zero_block))
    ahi[...] = jnp.zeros(ahi.shape, bf16)
    alo[...] = jnp.zeros(alo.shape, bf16)
    for i in range(TILE_DEV):
        for j in halo_of(i):
            put_a(j + HALF, i + HALF, le[tile_at(i, j)])
    on = forward(first_chunk)
    first_chunk[0].wait_recv()
    on.wait_recv()
    build_start(E_CHUNKS[0])
    for p, q in ((0, 2), (1, 2), (1, 3)):
        square(p, q)
    on = forward(second_chunk)
    second_chunk[0].wait_recv()
    on.wait_recv()
    build_start(E_CHUNKS[1])

    corners = [None, None]
    for p, q in ((0, 0), (0, 1), (1, 1)):
        square(p, q)
    own_parts([t for t in E_CHUNKS[0] if t[1] < HALF])
    for n, (a, b) in enumerate(LOW):
        sw[0, n] = lw[tile_at(a, b)]
    corners[1] = start(sw.at[0], rw.at[1], 13, (down, g))
    for p, q in ((2, 2), (2, 3), (3, 3)):
        square(p, q)
    own_parts([t for t in E_CHUNKS[0] if t[0] >= HALF])
    for n, (a, b) in enumerate(LOW):
        sw[1, n] = lw[tile_at(a + HALF, b + HALF)]
    corners[0] = start(sw.at[1], rw.at[0], 14, (up, g))
    own_parts([t for t in E_CHUNKS[0] if t[0] < HALF <= t[1]])

    chunks = []
    halos = (to_high, to_low)
    for side in range(2):
        halos[side].wait_recv()
        build_corner(re, side)
        halo_side(side)
        chunks.append(gather(fw, OWN + side * SIDE, SIDE, (10, 15)[side]))
    build_own_square()
    for i in range(TILE_DEV):
        for s in range(BAND):
            put_a(i + s, i + HALF, lw[i * BAND + s])
    eye = (
        lax.broadcasted_iota(jnp.int32, (width, TILE), 0) + g * width
        == lax.broadcasted_iota(jnp.int32, (width, TILE), 1)
    ).astype(f32)

    def second(i, s, acc):
        val = 1.5 * lw[i * BAND + s] - acc
        if s == HALF:
            val = val + 0.4375 * eye
        out[i, s] = val

    for half in range(2):
        on = forward(chunks[half])
        chunks[half][0].wait_recv()
        on.wait_recv()
        build_side(SIDES[half])
        corners[half].wait_recv()
        build_corner(rw, half)
        for p in (2 * half, 2 * half + 1):
            product(p, second)
    for item in pending:
        item.wait_send()


def whole_kernel(rows, cap, groups, scale, *refs):
    operands, out, dh, rh = refs[:8], refs[8], refs[9], refs[10]
    route_scratch, band_scratch = refs[11:26], refs[26:]
    route_kernel(rows, cap, groups, *operands, dh, rh, *route_scratch)
    band_kernel(rows, groups, scale, out, dh, rh, *band_scratch)


def local(edge_feats, edge_owner, src_local, band_slot, dst_local, w_first, w_second, w_third):
    groups = lax.axis_size("feat")
    rows = lax.axis_size("rows")
    edges = edge_feats.shape[0]
    cap = max(2, 2 * edges // rows)
    width = TILE // groups
    tiles = (NT, width, TILE)
    vm = pl.BlockSpec(memory_space=pltpu.VMEM)
    anywhere = pl.BlockSpec(memory_space=pl.ANY)
    operands = (
        edge_feats, edge_owner.reshape(1, edges), src_local.reshape(1, edges),
        band_slot.reshape(1, edges), dst_local.reshape(1, edges), w_first, w_second, w_third,
    )
    partners = rows * groups
    sums = pltpu.VMEM((NT * NB, BLOCK // groups * TILE), f32)
    degree = groups * edges / (TILE_DEV * NB)
    scale = 0.5 * (0.5 / math.sqrt(2.0 * BLOCK * degree))
    return pl.pallas_call(
        functools.partial(whole_kernel, rows, cap, groups, scale),
        out_shape=jax.ShapeDtypeStruct((TILE_DEV, BAND, width, TILE), f32),
        in_specs=[anywhere] * len(operands),
        out_specs=vm,
        scratch_shapes=[pltpu.VMEM(tiles, f32)] * 2
        + [pltpu.VMEM(item.shape, item.dtype) for item in operands]
        + [
            pltpu.VMEM((rows, groups, cap, LANES), f32),
            pltpu.VMEM((partners, cap, LANES), f32),
            sums,
            sums,
            pltpu.SemaphoreType.DMA((len(operands),)),
            pltpu.SemaphoreType.DMA((partners,)),
            pltpu.SemaphoreType.DMA((partners,)),
        ]
        + [pltpu.VMEM(tiles, f32)] * 2
        + [pltpu.VMEM((SENT, TILE, TILE), f32)] * 2
        + [pltpu.VMEM((2, PART, width, TILE), f32)] * 2
        + [pltpu.VMEM((2, CORNER, width, TILE), f32)] * 4
        + [pltpu.VMEM((WIN * TILE, TILE_DEV * TILE), bf16)] * 2
        + [pltpu.VMEM((TILE_DEV * TILE, WIN * TILE), bf16)] * 2
        + [pltpu.VMEM((WIN * width, WIN * TILE), bf16)] * 2
        + [pltpu.VMEM((len(HALO_SLOT), TILE, TILE), f32)]
        + [pltpu.VMEM((len(OWN_SLOT), TILE, TILE), f32)]
        + [pltpu.SemaphoreType.DMA((18,))] * 2,
        compiler_params=pltpu.CompilerParams(
            collective_id=0, has_side_effects=True, vmem_limit_bytes=60 << 20
        ),
    )(*operands)


def solution(mesh):
    in_specs = (
        P(("rows", "feat"), None),
        P(("rows", "feat"), None),
        P(("rows", "feat")),
        P(("rows", "feat")),
        P(("rows", "feat")),
        P(),
        P(),
        P(),
    )
    out_specs = P("rows", None, "feat", None)
    return jax.shard_map(local, mesh=mesh, in_specs=in_specs, out_specs=out_specs, check_vma=False)
```

```python
import functools
import math

import jax
import jax.numpy as jnp
from jax import lax
from jax.experimental import pallas as pl
from jax.experimental.pallas import tpu as pltpu
from jax.sharding import PartitionSpec as P

BLOCK = 16
TILE = 128
BAND = 9
TILE_DEV = 8
HALF = BAND // 2
NB = TILE // BLOCK
WIN = TILE_DEV + 2 * HALF
NT = TILE_DEV * BAND
LANES = 128
CODE_LANE = 112
MESH = pl.DeviceIdType.MESH
f32 = jnp.float32
bf16 = jnp.bfloat16


def split2(x):
    hi = x.astype(bf16)
    return hi, (x - hi.astype(f32)).astype(bf16)


def mm(a, b):
    return jnp.dot(a, b, preferred_element_type=f32)


def piece_columns(groups, cols):
    per = BLOCK * cols
    sub = cols * cols
    shape = (BLOCK * BLOCK, groups * LANES)
    source = lax.broadcasted_iota(jnp.int32, shape, 0)
    lane = lax.broadcasted_iota(jnp.int32, shape, 1)
    g, k = lane // LANES, lane % LANES
    other = (k - per) // sub
    other = other + (other >= g).astype(jnp.int32)
    from_row = other * per + g * sub + (k - per) % sub
    want = jnp.where(k < per, g * per + k, jnp.where(k < CODE_LANE, from_row, -1))
    return (source == want).astype(bf16)


def spread_columns(groups, cols, g):
    per = BLOCK * cols
    sub = cols * cols
    width = TILE // groups
    shape = (LANES, cols * TILE)
    source = lax.broadcasted_iota(jnp.int32, shape, 0)
    full = lax.broadcasted_iota(jnp.int32, shape, 1)
    u, lane = full // TILE, full % TILE
    other, unit = lane // width, lane % cols
    by_col = source == (other * cols + unit) * cols + u
    apart = per + (other - (other > g).astype(jnp.int32)) * sub + u * cols + unit
    by_row = source == jnp.where(other == g, (g * cols + u) * cols + unit, apart)
    return by_col.astype(bf16), by_row.astype(bf16)


def route_kernel(
    rows, cap, groups,
    feats_in, owner_in, src_in, slot_in, dst_in, w1_in, w2_in, w3_in, dh, rh,
    feats, owner_row, src_row, slot_row, dst_row, w1, w2, w3, sent, rec, acc_col, acc_row,
    sems, s_sem, r_sem,
):
    r = lax.axis_index("rows")
    g = lax.axis_index("feat")
    n = rows * groups
    edges = feats.shape[0]
    cols = BLOCK // groups
    width = TILE // groups

    def partner(q):
        turn = q // groups
        step = rows // 2 + (turn + 1) // 2 * (1 - 2 * (turn % 2))
        return (r + step + rows) % rows, (g + groups - 1 - q % groups) % groups

    def record_copy(q):
        to_row, to_group = partner(q)
        return pltpu.make_async_remote_copy(
            src_ref=sent.at[to_row, to_group], dst_ref=rec.at[q],
            send_sem=s_sem.at[q], recv_sem=r_sem.at[q],
            device_id=(to_row, to_group), device_id_type=MESH,
        )

    barrier = pltpu.get_barrier_semaphore()

    def greet(q, carry):
        pl.semaphore_signal(barrier, inc=1, device_id=partner(q), device_id_type=MESH)
        return carry

    lax.fori_loop(0, n - 1, greet, 0)

    fetches = []
    for k, (src, dst) in enumerate(
        (
            (feats_in, feats), (w1_in, w1), (w2_in, w2), (w3_in, w3), (owner_in, owner_row),
            (src_in, src_row), (slot_in, slot_row), (dst_in, dst_row),
        )
    ):
        fetch = pltpu.make_async_copy(src, dst, sems.at[k])
        fetch.start()
        fetches.append(fetch)
    perm = piece_columns(groups, cols)
    before = (
        lax.broadcasted_iota(jnp.int32, (edges, edges), 0)
        < lax.broadcasted_iota(jnp.int32, (edges, edges), 1)
    ).astype(bf16)
    for fetch in fetches:
        fetch.wait()
    h1 = mm(feats[...], w1[...])
    h1 = (h1 / (1.0 + jnp.exp(-h1))).astype(bf16)
    h2 = mm(h1, w2[...])
    h2 = (h2 / (1.0 + jnp.exp(-h2))).astype(bf16)
    w3p = mm(w3[...], perm).astype(bf16)
    vals = mm(h2, w3p)
    code = (8192 + src_row[...] * 128 + slot_row[...] * 8 + dst_row[...]).astype(f32)
    code_col = jnp.broadcast_to(code, (LANES, edges)).T[:, :1]
    lane = lax.broadcasted_iota(jnp.int32, vals.shape, 1)
    vals = jnp.where(lane % LANES == CODE_LANE, code_col, vals)
    owner = owner_row[...]
    names = (owner == lax.broadcasted_iota(jnp.int32, (rows, edges), 0)).astype(f32)
    rank = jnp.sum(names * mm(names.astype(bf16), before), axis=0, keepdims=True).astype(jnp.int32)
    target = owner * cap + rank
    place = (target == lax.broadcasted_iota(jnp.int32, (rows * cap, edges), 0)).astype(bf16)
    hi, lo = split2(vals)
    packed = mm(place, hi) + mm(place, lo)
    for k in range(groups):
        part = packed[:, k * LANES : (k + 1) * LANES]
        sent[:, k] = part.reshape(rows, cap, LANES)

    pl.semaphore_wait(barrier, n - 1)

    def send(q, carry):
        record_copy(q).start()
        return carry

    lax.fori_loop(0, n - 1, send, 0)
    rec[n - 1] = sent[r, g]

    by_col, by_row = spread_columns(groups, cols, g)
    spread_lane = lax.broadcasted_iota(jnp.int32, (1, cols * TILE), 1)
    lane_block = spread_lane % width // cols
    shares = 4
    size = n // shares
    line = lax.broadcasted_iota(jnp.int32, (NT * NB, size * cap), 0)

    def arrived(q, carry):
        record_copy(q).wait_recv()
        return carry

    for share in reversed(range(shares)):
        lax.fori_loop(share * size, min((share + 1) * size, n - 1), arrived, 0)
        x = rec[share * size : (share + 1) * size].reshape(size * cap, LANES)
        code_c = x[:, CODE_LANE : CODE_LANE + 1].astype(jnp.int32)
        code_r = x.T[CODE_LANE : CODE_LANE + 1, :].astype(jnp.int32)
        hi, lo = split2(x)
        tile_id = (
            lax.shift_right_logical(code_r, 10) % 8 * BAND + lax.shift_right_logical(code_r, 3) % 16
        )
        valid = code_r >= 8192
        src_r, dst_r = lax.shift_right_logical(code_r, 7) % 8, code_r % 8
        src_c, dst_c = lax.shift_right_logical(code_c, 7) % 8, code_c % 8
        for acc, spread, row_block, lane_of in (
            (acc_row, by_row, src_r, dst_c),
            (acc_col, by_col, dst_r, src_c),
        ):
            index = jnp.where(valid, tile_id * NB + row_block, -1)
            put = (line == index).astype(bf16)
            keep = lane_block == lane_of
            strips_hi = jnp.where(keep, mm(hi, spread), 0.0).astype(bf16)
            strips_lo = jnp.where(keep, mm(lo, spread), 0.0).astype(bf16)
            total = mm(put, strips_hi) + mm(put, strips_lo)
            if share == shares - 1:
                acc[...] = total
            else:
                acc[...] += total
    for dest, acc in ((rh, acc_row), (dh, acc_col)):
        for u in range(cols):
            dest[:, pl.ds(u, NB, stride=cols), :] = acc[:, u * TILE : (u + 1) * TILE].reshape(
                NT, NB, TILE
            )

    def sent_off(q, carry):
        record_copy(q).wait_send()
        return carry

    lax.fori_loop(0, n - 1, sent_off, 0)


def own_tiles():
    return [(i, j) for i in range(TILE_DEV) for j in range(TILE_DEV) if abs(i - j) <= HALF]


def tile_at(i, j):
    return i * BAND + j - i + HALF


LOW = [(a, b) for a in range(HALF) for b in range(HALF)]
LOW_PART = [(j, i) for j in range(HALF) for i in range(j - HALF, 0)]
HIGH_PART = [
    (j, i) for j in range(TILE_DEV - HALF, TILE_DEV) for i in range(TILE_DEV, j + HALF + 1)
]
CORNER = len(LOW)
PART = len(LOW_PART)
PAIRS = TILE_DEV // 2


def halo_of(i):
    return [j for j in range(i - HALF, i + HALF + 1) if not 0 <= j < TILE_DEV]


E_CHUNKS = [
    [t for t in own_tiles() if t[0] <= t[1]],
    [(i, j) for i in range(TILE_DEV) for j in halo_of(i)],
]
E_AT = {t: n for n, t in enumerate(sum(E_CHUNKS, []))}
SENT = len(E_AT)
OWN = len(E_CHUNKS[0])
SIDE = len(E_CHUNKS[1]) // 2
SIDES = [E_CHUNKS[1][:SIDE], E_CHUNKS[1][SIDE:]]
HALO_SLOT = {t: n for n, t in enumerate(E_CHUNKS[1])}
OWN_SLOT = {t: n for n, t in enumerate(t for t in E_CHUNKS[0] if t[0] != t[1])}


def band_kernel(
    rows, groups, scale, out,
    dh, rh, le, lw, fe, fw, sp, rp, se, re, sw, rw, bhi, blo, fhi, flo, ahi, alo, t1, tw, s_sem, r_sem,
):
    r = lax.axis_index("rows")
    g = lax.axis_index("feat")
    width = TILE // groups
    up, down = lax.rem(r + 1, rows), lax.rem(r + rows - 1, rows)
    y, c = g // 2, g % 2
    core_peer, y_peer = y * 2 + (1 - c), (1 - y) * 2 + c
    mine = pl.ds(pl.multiple_of(g * width, width), width)
    theirs = pl.ds(pl.multiple_of(y_peer * width, width), width)

    def copy(src, dst, sem, who):
        return pltpu.make_async_remote_copy(
            src_ref=src, dst_ref=dst, send_sem=s_sem.at[sem], recv_sem=r_sem.at[sem],
            device_id=who, device_id_type=MESH,
        )

    pending = []

    def start(*args):
        item = copy(*args)
        item.start()
        pending.append(item)
        return item

    def gather(buf, first, size, sem):
        part = buf.at[pl.ds(first, size), mine]
        near = start(part, part, sem, (r, core_peer))
        far = start(part, part, sem + 1, (r, y_peer))
        return near, far, buf.at[pl.ds(first, size), theirs], sem + 2

    def forward(item):
        item[1].wait_recv()
        return start(item[2], item[2], item[3], (r, core_peer))

    def put_a(jj, kk, val):
        h, l = split2(val)
        ahi[jj * width : (jj + 1) * width, kk * TILE : (kk + 1) * TILE] = h
        alo[jj * width : (jj + 1) * width, kk * TILE : (kk + 1) * TILE] = l

    def put(refs, row, col, parts):
        for ref, part in zip(refs, parts):
            ref[row * TILE : (row + 1) * TILE, col * TILE : (col + 1) * TILE] = part

    right, left = (bhi, blo), (fhi, flo)

    def build_corner(recv, side):
        at = 0 if side == 0 else WIN - HALF
        for n, (a, b) in enumerate(LOW):
            put_a(b + at, a + at, recv[side, n])

    def build_start(tiles):
        for i, j in tiles:
            full = fe[E_AT[i, j]]
            parts = split2(full)
            put(right, j + HALF, i, parts)
            inside = 0 <= j < TILE_DEV
            if inside:
                put(left, j, i + HALF, parts)
            if i != j:
                turned = split2(full.T)
                put(left, i, j + HALF, turned)
                if inside:
                    put(right, i + HALF, j, turned)

    def build_own_square():
        for i, j in E_CHUNKS[0]:
            put(right, j + HALF, i, split2(fw[E_AT[i, j]]))
            if i != j:
                put(right, i + HALF, j, split2(tw[OWN_SLOT[i, j]]))

    def build_side(tiles):
        for i, j in tiles:
            full = fw[E_AT[i, j]]
            put(right, j + HALF, i, split2(full))
            t1[HALO_SLOT[i, j]] = full.T
        for i, j in tiles:
            put_a(i + HALF, j + HALF, t1[HALO_SLOT[i, j], mine, :])

    def three(ref_l, at_l, ref_r, at_r):
        a_h, b_h = ref_l[0][at_l], ref_r[0][at_r]
        return mm(a_h, b_h) + mm(a_h, ref_r[1][at_r]) + mm(ref_l[1][at_l], b_h)

    def square(p, q):
        mid = slice(2 * q * TILE, (2 * p + 10) * TILE)
        acc = three(
            left, (slice(2 * q * TILE, (2 * q + 2) * TILE), mid),
            right, (mid, slice(2 * p * TILE, (2 * p + 2) * TILE)),
        )
        for di in range(2):
            for dj in range(2):
                i, j = 2 * p + di, 2 * q + dj
                if (i, j) in E_AT:
                    n = E_AT[i, j]
                    val = fe[n] + acc[dj * TILE : (dj + 1) * TILE, di * TILE : (di + 1) * TILE]
                    fw[n] = val
                    if i != j:
                        tw[OWN_SLOT[i, j]] = val.T

    def own_parts(tiles):
        for i, j in tiles:
            lw[tile_at(i, j)] = fw[E_AT[i, j], mine, :]
            if i != j:
                lw[tile_at(j, i)] = tw[OWN_SLOT[i, j], mine, :]

    def halo_side(side):
        jj0 = 0 if side == 0 else WIN - HALF
        mid = slice(0, TILE_DEV * TILE) if side == 0 else slice(TILE_DEV * TILE, WIN * TILE)
        i0 = 0 if side == 0 else TILE_DEV - HALF
        acc = three(
            (ahi, alo), (slice(jj0 * width, (jj0 + HALF) * width), mid),
            right, (mid, slice(i0 * TILE, (i0 + HALF) * TILE)),
        )
        for i, j in SIDES[side]:
            m = j + HALF - jj0
            val = le[tile_at(i, j)] + acc[
                m * width : (m + 1) * width, (i - i0) * TILE : (i - i0 + 1) * TILE
            ]
            lw[tile_at(i, j)] = val
            fw[E_AT[i, j], mine, :] = val

    def product(p, emit, inside):
        first, last = 2 * p, 2 * p + 10
        if inside:
            first, last = max(first, HALF), min(last, HALF + TILE_DEV)
        elif p < PAIRS // 2:
            last = HALF
        else:
            first = HALF + TILE_DEV
        mid = slice(2 * p * TILE, (2 * p + 10) * TILE)
        cols_at = slice(2 * p * TILE, (2 * p + 2) * TILE)
        acc = three((ahi, alo), (slice(first * width, last * width), mid), right, (mid, cols_at))
        for di in range(2):
            for s in range(BAND):
                m = 2 * p + di + s - first
                if 0 <= m < last - first:
                    emit(
                        2 * p + di, s,
                        acc[m * width : (m + 1) * width, di * TILE : (di + 1) * TILE],
                    )

    for n, (j, i) in enumerate(LOW_PART):
        sp[0, n] = rh[tile_at(j, i)]
    for n, (j, i) in enumerate(HIGH_PART):
        sp[1, n] = rh[tile_at(j, i)]
    part_low = start(sp.at[0], rp.at[1], 0, (down, g))
    part_high = start(sp.at[1], rp.at[0], 1, (up, g))
    for i, j in own_tiles():
        val = scale * (dh[tile_at(i, j)] + rh[tile_at(j, i)])
        le[tile_at(i, j)] = val
        if i <= j:
            fe[E_AT[i, j], mine, :] = val
    first_chunk = gather(fe, 0, len(E_CHUNKS[0]), 2)
    for n, (a, b) in enumerate(LOW):
        se[0, n] = le[tile_at(a, b)]
        se[1, n] = le[tile_at(a + HALF, b + HALF)]
    part_low.wait_recv()
    part_high.wait_recv()
    for n, (j, i) in enumerate(HIGH_PART):
        own, halo = i - TILE_DEV, j - TILE_DEV
        val = scale * (dh[tile_at(own, halo)] + rp[0, n])
        le[tile_at(own, halo)] = val
        fe[E_AT[own, halo], mine, :] = val
    for n, (j, i) in enumerate(LOW_PART):
        own, halo = i + TILE_DEV, j + TILE_DEV
        val = scale * (dh[tile_at(own, halo)] + rp[1, n])
        le[tile_at(own, halo)] = val
        fe[E_AT[own, halo], mine, :] = val
    second_chunk = gather(fe, len(E_CHUNKS[0]), len(E_CHUNKS[1]), 5)
    to_low = start(se.at[0], re.at[1], 8, (down, g))
    to_high = start(se.at[1], re.at[0], 9, (up, g))

    zero_block = jnp.zeros((TILE, TILE), bf16)
    empty = set()
    for p in range(PAIRS):
        empty |= {(2 * p + 9, 2 * p), (2 * p, 2 * p + 1)}
    for i in range(HALF):
        empty |= {(kk, i) for kk in range(i)}
        empty |= {(kk, i + HALF) for kk in range(i + HALF + BAND, WIN)}
    for kk, i in sorted(empty):
        put(right, kk, i, (zero_block, zero_block))
    for p in range(PAIRS):
        put(left, 2 * p, 2 * p + 9, (zero_block, zero_block))
        put(left, 2 * p + 1, 2 * p, (zero_block, zero_block))
    ahi[...] = jnp.zeros(ahi.shape, bf16)
    alo[...] = jnp.zeros(alo.shape, bf16)
    for i in range(TILE_DEV):
        for j in halo_of(i):
            put_a(j + HALF, i + HALF, le[tile_at(i, j)])
    on = forward(first_chunk)
    first_chunk[0].wait_recv()
    on.wait_recv()
    build_start(E_CHUNKS[0])
    for p, q in ((0, 2), (1, 2), (1, 3)):
        square(p, q)
    on = forward(second_chunk)
    second_chunk[0].wait_recv()
    on.wait_recv()
    build_start(E_CHUNKS[1])

    corners = [None, None]
    for p, q in ((0, 0), (0, 1), (1, 1)):
        square(p, q)
    own_parts([t for t in E_CHUNKS[0] if t[1] < HALF])
    for n, (a, b) in enumerate(LOW):
        sw[0, n] = lw[tile_at(a, b)]
    corners[1] = start(sw.at[0], rw.at[1], 13, (down, g))
    for p, q in ((2, 2), (2, 3), (3, 3)):
        square(p, q)
    own_parts([t for t in E_CHUNKS[0] if t[0] >= HALF])
    for n, (a, b) in enumerate(LOW):
        sw[1, n] = lw[tile_at(a + HALF, b + HALF)]
    corners[0] = start(sw.at[1], rw.at[0], 14, (up, g))
    own_parts([t for t in E_CHUNKS[0] if t[0] < HALF <= t[1]])

    chunks = [None, None]
    halos = (to_high, to_low)
    for side in (1, 0):
        halos[side].wait_recv()
        build_corner(re, side)
        halo_side(side)
        chunks[side] = gather(fw, OWN + side * SIDE, SIDE, (10, 15)[side])
    build_own_square()
    for i in range(TILE_DEV):
        for s in range(BAND):
            put_a(i + s, i + HALF, lw[i * BAND + s])
    eye = (
        lax.broadcasted_iota(jnp.int32, (width, TILE), 0) + g * width
        == lax.broadcasted_iota(jnp.int32, (width, TILE), 1)
    ).astype(f32)

    def second(i, s, acc):
        val = 1.5 * lw[i * BAND + s] - acc
        if s == HALF:
            val = val + 0.4375 * eye
        out[i, s] = val

    for half in (1, 0):
        on = forward(chunks[half])
        chunks[half][0].wait_recv()
        on.wait_recv()
        build_side(SIDES[half])
        for p in (2 * half, 2 * half + 1):
            product(p, second, True)
    for half in (1, 0):
        corners[half].wait_recv()
        build_corner(rw, half)
        for p in (2 * half, 2 * half + 1):
            product(p, second, False)
    for item in pending:
        item.wait_send()


def whole_kernel(rows, cap, groups, scale, *refs):
    operands, out, dh, rh = refs[:8], refs[8], refs[9], refs[10]
    route_scratch, band_scratch = refs[11:26], refs[26:]
    route_kernel(rows, cap, groups, *operands, dh, rh, *route_scratch)
    band_kernel(rows, groups, scale, out, dh, rh, *band_scratch)


def local(edge_feats, edge_owner, src_local, band_slot, dst_local, w_first, w_second, w_third):
    groups = lax.axis_size("feat")
    rows = lax.axis_size("rows")
    edges = edge_feats.shape[0]
    cap = max(2, 2 * edges // rows)
    width = TILE // groups
    tiles = (NT, width, TILE)
    vm = pl.BlockSpec(memory_space=pltpu.VMEM)
    anywhere = pl.BlockSpec(memory_space=pl.ANY)
    operands = (
        edge_feats, edge_owner.reshape(1, edges), src_local.reshape(1, edges),
        band_slot.reshape(1, edges), dst_local.reshape(1, edges), w_first, w_second, w_third,
    )
    partners = rows * groups
    sums = pltpu.VMEM((NT * NB, BLOCK // groups * TILE), f32)
    degree = groups * edges / (TILE_DEV * NB)
    scale = 0.5 * (0.5 / math.sqrt(2.0 * BLOCK * degree))
    return pl.pallas_call(
        functools.partial(whole_kernel, rows, cap, groups, scale),
        out_shape=jax.ShapeDtypeStruct((TILE_DEV, BAND, width, TILE), f32),
        in_specs=[anywhere] * len(operands),
        out_specs=vm,
        scratch_shapes=[pltpu.VMEM(tiles, f32)] * 2
        + [pltpu.VMEM(item.shape, item.dtype) for item in operands]
        + [
            pltpu.VMEM((rows, groups, cap, LANES), f32),
            pltpu.VMEM((partners, cap, LANES), f32),
            sums,
            sums,
            pltpu.SemaphoreType.DMA((len(operands),)),
            pltpu.SemaphoreType.DMA((partners,)),
            pltpu.SemaphoreType.DMA((partners,)),
        ]
        + [pltpu.VMEM(tiles, f32)] * 2
        + [pltpu.VMEM((SENT, TILE, TILE), f32)] * 2
        + [pltpu.VMEM((2, PART, width, TILE), f32)] * 2
        + [pltpu.VMEM((2, CORNER, width, TILE), f32)] * 4
        + [pltpu.VMEM((WIN * TILE, TILE_DEV * TILE), bf16)] * 2
        + [pltpu.VMEM((TILE_DEV * TILE, WIN * TILE), bf16)] * 2
        + [pltpu.VMEM((WIN * width, WIN * TILE), bf16)] * 2
        + [pltpu.VMEM((len(HALO_SLOT), TILE, TILE), f32)]
        + [pltpu.VMEM((len(OWN_SLOT), TILE, TILE), f32)]
        + [pltpu.SemaphoreType.DMA((18,))] * 2,
        compiler_params=pltpu.CompilerParams(
            collective_id=0, has_side_effects=True, vmem_limit_bytes=60 << 20
        ),
    )(*operands)


def solution(mesh):
    in_specs = (
        P(("rows", "feat"), None),
        P(("rows", "feat"), None),
        P(("rows", "feat")),
        P(("rows", "feat")),
        P(("rows", "feat")),
        P(),
        P(),
        P(),
    )
    out_specs = P("rows", None, "feat", None)
    return jax.shard_map(local, mesh=mesh, in_specs=in_specs, out_specs=out_specs, check_vma=False)
```
